256 devices in a mesh: dom: 64 (over y, z, core), tile: 4 (over x).
Axes of the slice: x: 4, y: 4, z: 8, core: 2. Of those that a mesh axis runs over, the one named last changes fastest.
Arguments:
- tile_latent: bfloat16 [32768, 512], P(('dom', 'tile')), may hold values from -6 to 6
- relay_pick: int32 [256, 128], P(('dom', 'tile')), may hold values from 0 to 127, as said below
- relay_from: int32 [32768], P(('dom', 'tile')), may hold values from 0 to 255, as said below
- cut_pick: int32 [256, 32], P(('dom', 'tile')), may hold values from 0 to 127, as said below
- edge_latent: bfloat16 [196608, 512], P(('dom', 'tile')), may hold values from -6 to 6
- edge_sender: int32 [196608], P(('dom', 'tile')), may hold values from 0 to 543, as said below
- edge_receiver: int32 [196608], P(('dom', 'tile')), may hold values from 0 to 127, as said below
- edge_in: bfloat16 [1536, 512], replicated, may hold values from -0.15625 to 0.15625
- edge_out: bfloat16 [512, 512], replicated
- node_in: bfloat16 [1024, 512], replicated, may hold values from -0.1875 to 0.1875
- node_out: bfloat16 [512, 512], replicated
- node_cot: bfloat16 [32768, 512], P(('dom', 'tile')), may hold values from -6 to 6
- edge_cot: bfloat16 [196608, 512], P(('dom', 'tile')), may hold values from -6 to 6
Outputs:
- node_update: bfloat16 [32768, 512], P(('dom', 'tile'))
- edge_update: bfloat16 [196608, 512], P(('dom', 'tile'))
- latent_grad: bfloat16 [32768, 512], P(('dom', 'tile'))
- edge_grad: bfloat16 [196608, 512], P(('dom', 'tile'))
- weight_grad: float32 [3584, 512], P('dom', 'tile')
The draws below stay inside these ranges and needn't reach their ends.
Inputs may be any that keep to these rules, and one draw needn't show every extreme that they name: `relay_pick`: slot j of the block for partition q on device (p, t) carries a row when j is under that pair's count; the counts depend on the partition offset q - p and are 2 or half of it, zero for q = p; the other slots name rows that no one reads. No tile row goes out twice, and the rows that go out nowhere stay on their device. `relay_from`: each device's block names 128 distinct places: its own staying tile rows (below 128) or received slots that carry a row, 128 + s * 2 + j for slot j from partition s. `cut_pick`: distinct rows within a device. `edge_sender`: below 512: a node of the device's own partition; above: a halo slot, first the 16 from the lower partition, then the 16 from the upper. `edge_receiver`: not falling within a device.
All inputs are finite; a program needn't handle non-finite values.
Results may differ from the reference program's by a relative error of at most 0.013.
Values may be sent and summed in bfloat16 or wider, within the bound.
A program may use at most 128 MiB of HBM per device.

```python
import math
import jax
import jax.numpy as jnp
from jax import lax

H = 512
NODE_DEV = 128
EDGE_DEV = 768
RELAY_CAP = 2
HALO_CAP = 16
NODES = 32768
EDGES = 196608
N_DOM = 64
N_TILE = 4


def relay_plan(key):
    device_count = N_DOM * N_TILE
    span = NODE_DEV + N_DOM * RELAY_CAP
    row_order = jax.vmap(lambda subkey: jax.random.permutation(subkey, NODE_DEV))(jax.random.split(jax.random.fold_in(key, 101), device_count)).astype(jnp.int32).reshape(N_DOM, N_TILE, NODE_DEV)
    ranking = jax.vmap(lambda subkey: jax.random.permutation(subkey, N_DOM - 1))(jax.random.split(jax.random.fold_in(key, 102), N_TILE)).astype(jnp.int32)
    counts = jnp.where(ranking % 2 == 0, RELAY_CAP, RELAY_CAP // 2).astype(jnp.int32)
    counts = jnp.concatenate([jnp.zeros((N_TILE, 1), jnp.int32), counts], 1)
    starts = jnp.cumsum(counts, 1) - counts
    staying = NODE_DEV - jnp.sum(counts, 1)
    source = jnp.arange(N_DOM, dtype=jnp.int32)[:, None, None, None]
    column = jnp.arange(N_TILE, dtype=jnp.int32)[None, :, None, None]
    target = jnp.arange(N_DOM, dtype=jnp.int32)[None, None, :, None]
    slot_index = jnp.arange(RELAY_CAP, dtype=jnp.int32)[None, None, None, :]
    offset = (target - source) % N_DOM
    is_live = slot_index < counts[column, offset]
    position = jnp.clip(staying[column] + starts[column, offset] + slot_index, 0, NODE_DEV - 1)
    chosen = jnp.where(is_live, position, slot_index % NODE_DEV)
    chosen = jnp.broadcast_to(chosen, (N_DOM, N_TILE, N_DOM, RELAY_CAP)).reshape(N_DOM, N_TILE, N_DOM * RELAY_CAP)
    pick_list = jnp.take_along_axis(row_order, chosen, axis=2).reshape(device_count, N_DOM * RELAY_CAP)
    inverse = jnp.argsort(row_order, axis=2).astype(jnp.int32)
    own_valid = inverse < staying[None, :, None]
    got = slot_index < counts[column, (source - target) % N_DOM]
    got = jnp.broadcast_to(got, (N_DOM, N_TILE, N_DOM, RELAY_CAP)).reshape(N_DOM, N_TILE, N_DOM * RELAY_CAP)
    is_valid = jnp.concatenate([jnp.broadcast_to(own_valid, (N_DOM, N_TILE, NODE_DEV)), got], 2)
    shuffle = jax.vmap(lambda subkey: jax.random.permutation(subkey, span))(jax.random.split(jax.random.fold_in(key, 103), device_count)).astype(jnp.int32).reshape(N_DOM, N_TILE, span)
    sort_score = jnp.where(is_valid, shuffle, shuffle + span)
    from_list = jnp.argsort(sort_score, axis=2)[:, :, :NODE_DEV].astype(jnp.int32)
    return (pick_list, from_list.reshape(-1))


def draw_relay_pick(key, part):
    plan = relay_plan(key)
    return plan[0]


def draw_relay_from(key, part):
    plan = relay_plan(key)
    return plan[1]


def draw_cut_pick(key, part):
    key = jax.random.fold_in(key, 3)
    subkeys = jax.random.split(key, N_DOM * N_TILE)
    return jax.vmap(lambda subkey: jax.random.permutation(subkey, NODE_DEV)[:2 * HALO_CAP])(subkeys).astype(jnp.int32)


def draw_edge_receiver(key, part):
    key = jax.random.fold_in(key, 5)
    drawn = jax.random.randint(key, (N_DOM * N_TILE, EDGE_DEV), 0, NODE_DEV, dtype=jnp.int32)
    return jnp.sort(drawn, axis=1).reshape(-1).astype(jnp.int32)


def draw_edge_sender(key, part):
    key = jax.random.fold_in(key, 7)
    subkeys = jax.random.split(key, 6)
    device_count = N_DOM * N_TILE
    part_rows = N_TILE * NODE_DEV
    used_rows = jax.random.randint(subkeys[0], (N_DOM * N_TILE * 2,), HALO_CAP // 2, HALO_CAP + 1, dtype=jnp.int32)
    forced = jax.random.randint(subkeys[1], (), 0, N_DOM * N_TILE * 2, dtype=jnp.int32)
    used_rows = used_rows.at[forced].set(HALO_CAP).reshape(N_DOM, N_TILE, 2)
    from_lower = jnp.roll(used_rows[:, :, 1], 1, axis=0).reshape(device_count, 1)
    from_upper = jnp.roll(used_rows[:, :, 0], -1, axis=0).reshape(device_count, 1)
    side_pick = jax.random.randint(subkeys[2], (device_count, EDGE_DEV), 0, 2, dtype=jnp.int32)
    slot_limit = jnp.where(side_pick == 0, from_lower, from_upper)
    slot_index = jax.random.randint(subkeys[3], (device_count, EDGE_DEV), 0, slot_limit, dtype=jnp.int32)
    is_cut = jax.random.randint(subkeys[4], (device_count, EDGE_DEV), 0, 4, dtype=jnp.int32) == 0
    inner_rows = jax.random.randint(subkeys[5], (device_count, EDGE_DEV), 0, part_rows, dtype=jnp.int32)
    return jnp.where(is_cut, part_rows + side_pick * HALO_CAP + slot_index, inner_rows).reshape(-1).astype(jnp.int32)


def draw_edge_out(key, part):
    key = jax.random.fold_in(key, 11)
    subkeys = jax.random.split(key, 2)
    base_vals = jax.random.normal(subkeys[0], (H, H), jnp.float32)
    col_scale = jnp.exp(jax.random.uniform(subkeys[1], (1, H), jnp.float32, math.log(0.3), math.log(3.0)))
    return (base_vals * col_scale * H ** (-0.5)).astype(jnp.bfloat16)


def draw_node_out(key, part):
    key = jax.random.fold_in(key, 13)
    subkeys = jax.random.split(key, 2)
    base_vals = jax.random.normal(subkeys[0], (H, H), jnp.float32)
    col_scale = jnp.exp(jax.random.uniform(subkeys[1], (1, H), jnp.float32, math.log(0.3), math.log(3.0)))
    return (base_vals * col_scale * H ** (-0.5)).astype(jnp.bfloat16)


def shard_levels(rng, dims, cuts, smallest, high):
    gain = 1.0
    for axis_at, parts in cuts:
        draws = jax.random.uniform(jax.random.fold_in(jax.random.fold_in(rng, 6), axis_at), (parts,), jnp.float32, smallest / len(cuts), high / len(cuts))
        gain = gain * jnp.repeat(jnp.exp(draws), dims[axis_at] // parts).reshape((-1,) + (1,) * (len(dims) - 1 - axis_at))
    return gain


def noise(stream_key, shape, width, bound, pieces=(), held_as=jnp.bfloat16):
    gain = shard_levels(stream_key, shape, pieces, -0.22, 0.18) if pieces else 1.0
    result = jax.random.normal(stream_key, shape, jnp.float32) * width * gain
    return jnp.minimum(jnp.maximum(result, -bound), bound).astype(held_as)


def setup_inputs(seed: int = 0) -> dict:
    keys = jax.random.split(jax.random.key(seed), 14)
    return {
        "tile_latent": noise(keys[0], (NODES, H), 1.0, 6.0, ((0, 256),)),
        "relay_pick": draw_relay_pick(jax.random.fold_in(keys[13], 71), 0),
        "relay_from": draw_relay_from(jax.random.fold_in(keys[13], 71), 0),
        "cut_pick": draw_cut_pick(jax.random.fold_in(keys[13], 71), 0),
        "edge_latent": noise(keys[4], (EDGES, H), 1.0, 6.0, ((0, 256),)),
        "edge_sender": draw_edge_sender(jax.random.fold_in(keys[13], 71), 0),
        "edge_receiver": draw_edge_receiver(jax.random.fold_in(keys[13], 71), 0),
        "edge_in": noise(keys[7], (3 * H, H), (3 * H) ** -0.5, 0.15625),
        "edge_out": draw_edge_out(jax.random.fold_in(keys[13], 71), 0),
        "node_in": noise(keys[9], (2 * H, H), (2 * H) ** -0.5, 0.1875),
        "node_out": draw_node_out(jax.random.fold_in(keys[13], 71), 0),
        "node_cot": noise(keys[11], (NODES, H), 1.0, 6.0, ((0, 256),)),
        "edge_cot": noise(keys[12], (EDGES, H), 1.0, 6.0, ((0, 256),)),
    }


EPSILON = 1e-05

def layer_norm(values):
    center = values - lax.optimization_barrier(jnp.mean(values, -1, keepdims=True))
    inverse = lax.rsqrt(lax.optimization_barrier(jnp.mean(center * center, -1, keepdims=True)) + EPSILON)
    return (center * inverse, inverse)

def norm_grad(normed, inverse, upstream):
    mean_up = lax.optimization_barrier(jnp.mean(upstream, -1, keepdims=True))
    mean_cross = lax.optimization_barrier(jnp.mean(upstream * normed, -1, keepdims=True))
    return inverse * (upstream - mean_up - normed * mean_cross)

def silu_grad(values):
    sigmoid = jax.nn.sigmoid(values)
    return sigmoid * (1.0 + values * (1.0 - sigmoid))

def flat_dot(left_mat, right_mat):
    return jnp.dot(left_mat, right_mat, preferred_element_type=jnp.float32)

def inner_dot(left_mat, right_mat):
    return lax.dot_general(left_mat, right_mat, (((0,), (0,)), ((), ())), preferred_element_type=jnp.float32)

def outer_dot(left_mat, right_mat):
    return lax.dot_general(left_mat, right_mat, (((1,), (1,)), ((), ())), preferred_element_type=jnp.float32)

def local_block(latent, row_table, edge_lat, senders, receivers, edge_in, edge_out, node_in, node_out, node_grad_in, edge_grad_in):
    feat_dim = edge_out.shape[0]
    node_count = latent.shape[0]
    w_edge = edge_in[:feat_dim]
    w_send = edge_in[feat_dim:2 * feat_dim]
    w_recv = edge_in[2 * feat_dim:]
    w_node = node_in[:feat_dim]
    w_agg = node_in[feat_dim:]
    send_rows = jnp.take(row_table, senders, axis=0)
    recv_rows = jnp.take(latent, receivers, axis=0)
    recv_proj = flat_dot(latent, w_recv)
    edge_pre = flat_dot(edge_lat, w_edge) + flat_dot(send_rows, w_send) + jnp.take(recv_proj, receivers, axis=0)
    edge_act = jax.nn.silu(edge_pre).astype(jnp.bfloat16)
    edge_lin = flat_dot(edge_act, edge_out)
    edge_normed, edge_inv = layer_norm(edge_lin)
    edge_new = (edge_lat.astype(jnp.float32) + edge_normed).astype(jnp.bfloat16)
    incidence = (receivers[:, None] == jnp.arange(node_count, dtype=jnp.int32)[None, :]).astype(jnp.bfloat16)
    aggregate = inner_dot(incidence, edge_new).astype(jnp.bfloat16)
    node_pre = flat_dot(latent, w_node) + flat_dot(aggregate, w_agg)
    node_act = jax.nn.silu(node_pre).astype(jnp.bfloat16)
    node_lin = flat_dot(node_act, node_out)
    node_normed, node_inv = layer_norm(node_lin)
    node_new = (latent.astype(jnp.float32) + node_normed).astype(jnp.bfloat16)
    node_upstream = node_grad_in.astype(jnp.float32)
    node_lin_grad = norm_grad(node_normed, node_inv, node_upstream).astype(jnp.bfloat16)
    grad_node_out = inner_dot(node_act, node_lin_grad)
    node_pre_grad = (outer_dot(node_lin_grad, node_out) * silu_grad(node_pre)).astype(jnp.bfloat16)
    grad_node_in = jnp.concatenate([inner_dot(latent, node_pre_grad), inner_dot(aggregate, node_pre_grad)], 0)
    node_direct = node_upstream + outer_dot(node_pre_grad, w_node)
    agg_grad = outer_dot(node_pre_grad, w_agg)
    edge_up = edge_grad_in.astype(jnp.float32) + jnp.take(agg_grad, receivers, axis=0)
    edge_lin_grad = norm_grad(edge_normed, edge_inv, edge_up).astype(jnp.bfloat16)
    grad_edge_out = inner_dot(edge_act, edge_lin_grad)
    edge_pre_grad = (outer_dot(edge_lin_grad, edge_out) * silu_grad(edge_pre)).astype(jnp.bfloat16)
    edge_grad = (edge_up + outer_dot(edge_pre_grad, w_edge)).astype(jnp.bfloat16)
    recv_grad = jax.ops.segment_sum(outer_dot(edge_pre_grad, w_recv), receivers, node_count)
    node_local = node_direct + recv_grad
    table_grad = jax.ops.segment_sum(outer_dot(edge_pre_grad, w_send), senders, row_table.shape[0])
    grad_edge_in = jnp.concatenate([inner_dot(edge_lat, edge_pre_grad), inner_dot(send_rows, edge_pre_grad), inner_dot(recv_rows, edge_pre_grad)], 0)
    weight_grad = jnp.concatenate([grad_edge_in, grad_edge_out, grad_node_in, grad_node_out], 0)
    return (node_new, edge_new, edge_grad, node_local, table_grad, weight_grad)

def reference(tile_latent, relay_pick, relay_from, cut_pick, edge_latent, edge_sender, edge_receiver, edge_in, edge_out, node_in, node_out, node_cot, edge_cot):
    feat_dim = H
    device_count = N_DOM * N_TILE
    part_count = N_TILE * NODE_DEV
    tile_grid = tile_latent.reshape(N_DOM, N_TILE, NODE_DEV, feat_dim)
    pick_list = relay_pick.reshape(N_DOM, N_TILE, N_DOM * RELAY_CAP)
    outgoing = jnp.take_along_axis(tile_grid, pick_list[..., None], axis=2).reshape(N_DOM, N_TILE, N_DOM, RELAY_CAP, feat_dim)
    incoming = jnp.transpose(outgoing, (2, 1, 0, 3, 4)).reshape(N_DOM, N_TILE, N_DOM * RELAY_CAP, feat_dim)
    pooled = jnp.concatenate([tile_grid, incoming], 2)
    places = relay_from.reshape(N_DOM, N_TILE, NODE_DEV)
    latent = jnp.take_along_axis(pooled, places[..., None], axis=2)
    cut_lists = cut_pick.reshape(N_DOM, N_TILE, 2 * HALO_CAP)
    cut_rows = jnp.take_along_axis(latent, cut_lists[..., None], axis=2).reshape(N_DOM, N_TILE, 2, HALO_CAP, feat_dim)
    from_lower = jnp.roll(cut_rows[:, :, 1], 1, axis=0)
    from_upper = jnp.roll(cut_rows[:, :, 0], -1, axis=0)
    partition = jnp.broadcast_to(latent.reshape(N_DOM, 1, part_count, feat_dim), (N_DOM, N_TILE, part_count, feat_dim))
    row_table = jnp.concatenate([partition, from_lower, from_upper], 2)
    stacked = (latent.reshape(device_count, NODE_DEV, feat_dim), row_table.reshape(device_count, part_count + 2 * HALO_CAP, feat_dim), edge_latent.reshape(device_count, EDGE_DEV, feat_dim), edge_sender.reshape(device_count, EDGE_DEV), edge_receiver.reshape(device_count, EDGE_DEV), node_cot.reshape(device_count, NODE_DEV, feat_dim), edge_cot.reshape(device_count, EDGE_DEV, feat_dim))

    def device_step(grad_total, device_item):
        local_out = local_block(device_item[0], device_item[1], device_item[2], device_item[3], device_item[4], edge_in, edge_out, node_in, node_out, device_item[5], device_item[6])
        return (grad_total + local_out[5], local_out[:5])
    grad_total, results = lax.scan(device_step, jnp.zeros((7 * feat_dim, feat_dim), jnp.float32), stacked)
    node_new, edge_new, edge_grad, node_local, table_grad = results
    part_grad = lax.optimization_barrier(jnp.sum(table_grad[:, :part_count].reshape(N_DOM, N_TILE, N_TILE, NODE_DEV, feat_dim), axis=1))
    lower_grad = table_grad[:, part_count:part_count + HALO_CAP].reshape(N_DOM, N_TILE, HALO_CAP, feat_dim)
    upper_grad = table_grad[:, part_count + HALO_CAP:].reshape(N_DOM, N_TILE, HALO_CAP, feat_dim)
    back_lower = jnp.roll(upper_grad, 1, axis=0)
    back_upper = jnp.roll(lower_grad, -1, axis=0)
    returned = jnp.concatenate([back_lower, back_upper], 2).reshape(device_count, 2 * HALO_CAP, feat_dim)
    halo_part = jax.vmap(lambda values_in, indices: jax.ops.segment_sum(values_in, indices, NODE_DEV))(returned, cut_lists.reshape(device_count, 2 * HALO_CAP))
    node_total = node_local + part_grad.reshape(device_count, NODE_DEV, feat_dim) + halo_part
    node_grad = node_total.astype(jnp.bfloat16)
    pool_grad = jax.vmap(lambda values_in, indices: jnp.zeros((NODE_DEV + N_DOM * RELAY_CAP, feat_dim), jnp.bfloat16).at[indices].set(values_in))(node_grad, places.reshape(device_count, NODE_DEV))
    stay_grad = pool_grad[:, :NODE_DEV]
    slot_grad = pool_grad[:, NODE_DEV:].reshape(N_DOM, N_TILE, N_DOM, RELAY_CAP, feat_dim)
    sent_grad = jnp.transpose(slot_grad, (2, 1, 0, 3, 4)).reshape(device_count, N_DOM * RELAY_CAP, feat_dim)
    tile_grad = jax.vmap(lambda base_rows, values_in, indices: base_rows.at[indices].add(values_in))(stay_grad, sent_grad, pick_list.reshape(device_count, N_DOM * RELAY_CAP))
    return (node_new.reshape(NODES, feat_dim), edge_new.reshape(EDGES, feat_dim), tile_grad.reshape(NODES, feat_dim), edge_grad.reshape(EDGES, feat_dim), grad_total)
```

```python
import jax
import jax.numpy as jnp
from jax import lax
from jax.experimental import pallas as pl
from jax.experimental.pallas import tpu as pltpu
from jax.sharding import PartitionSpec as P

EPSILON = 1e-05
MESH = pl.DeviceIdType.MESH
F32 = jnp.float32
BF16 = jnp.bfloat16
NX, NY, NZ, NC = 4, 4, 8, 2
DOM = NY * NZ * NC
H = 512
ND = 128
ED = 768
EB = 256
TR = 640
LN = 128


def iota(shape, dim):
    return lax.broadcasted_iota(jnp.int32, shape, dim)


def onehot(mask):
    return jnp.where(mask, 1.0, 0.0).astype(BF16)


def dot(a, b):
    return lax.dot_general(a, b, (((1,), (0,)), ((), ())), preferred_element_type=F32)


def dot_nt(a, b):
    return lax.dot_general(a, b, (((1,), (1,)), ((), ())), preferred_element_type=F32)


def dot_tn(a, b):
    return lax.dot_general(a, b, (((0,), (0,)), ((), ())), preferred_element_type=F32)


def norm(v):
    center = v - jnp.mean(v, -1, keepdims=True)
    inv = lax.rsqrt(jnp.mean(center * center, -1, keepdims=True) + EPSILON)
    return center * inv, inv


def norm_grad(normed, inv, up):
    mean_up = jnp.mean(up, -1, keepdims=True)
    mean_cross = jnp.mean(up * normed, -1, keepdims=True)
    return inv * (up - mean_up - normed * mean_cross)


def silu_pair(v):
    sig = 1.0 / (1.0 + jnp.exp(-v))
    act = v * sig
    return act, sig + act * (1.0 - sig)


def hi_lo(v):
    hi = v.astype(BF16)
    return hi, (v - hi.astype(F32)).astype(BF16)


def kernel(
    tile_ref, pick_ref, from_ref, cut_ref, snd_ref, rcv_ref, ncot_ref,
    e_hbm, cot_hbm, ein_hbm, eout_hbm, nin_hbm, nout_hbm,
    nodeup_ref, edgeup_hbm, latgrad_ref, edgegrad_hbm, wgrad_ref,
    e, cot, ein, eout, nin, nout, lsem,
    msg, inc, msgb, incb, table, lat, halo_s,
    sel_s, sel_st, sel_r, sel_rt, gat_i, back_o, back_p,
    pre, act, dsilu, normed, einv, enew, egrad, plg, ppg,
    gsum, gs, gr, hb, wg,
    csend, crecv, chip, rx, bx, ry, ry1, b1, rx1, zown, zp, rz,
    r_s, r_r, a_s, a_r, rb_s, rb_r, g_s, g_r, c_s, c_r, s2_s, s2_r, s3_s, s3_r, z_s, z_r,
):
    p = lax.axis_index("dom")
    x = lax.axis_index("tile")
    core = lax.rem(p, NC)
    z = lax.rem(p // NC, NZ)
    y = p // (NC * NZ)
    up = lax.rem(p + 1, DOM)
    dn = lax.rem(p + DOM - 1, DOM)
    sib = p + 1 - 2 * core

    def xpeer(j):
        return lax.rem(x + j, NX)

    def remote(src, dst, ss, rs, d, t):
        return pltpu.make_async_remote_copy(
            src, dst, ss, rs, device_id=(d, t), device_id_type=MESH
        )

    barrier = pltpu.get_barrier_semaphore()

    def greet(i, carry):
        pl.semaphore_signal(
            barrier, 1, device_id=(lax.rem(p + i, DOM), x), device_id_type=MESH
        )
        return carry

    lax.fori_loop(1, DOM, greet, 0)
    for j in range(1, NX):
        pl.semaphore_signal(barrier, 1, device_id=(p, xpeer(j)), device_id_type=MESH)

    loads = [
        pltpu.make_async_copy(s, d, lsem.at[i])
        for i, (s, d) in enumerate(
            (
                (e_hbm, e), (ein_hbm, ein), (eout_hbm, eout), (nin_hbm, nin),
                (nout_hbm, nout), (cot_hbm, cot),
            )
        )
    ]
    for c in loads:
        c.start()

    pickb = jnp.broadcast_to(pick_ref[...], (ND, LN)).astype(F32).astype(BF16)
    quad = onehot(iota((4 * LN, LN), 0) // 4 == iota((4 * LN, LN), 1))
    rep = dot_nt(quad, pickb)
    qlane = iota((4 * LN, LN), 1).astype(F32)
    qmod = iota((4 * LN, LN), 0) % 4
    out = jnp.zeros((4 * LN, LN), F32)
    for c in range(4):
        out += dot(
            onehot((rep == qlane) & (qmod == c)), tile_ref[:, c * LN : (c + 1) * LN]
        )
    msg[...] = out.reshape(DOM, 8, LN).astype(BF16)
    inc[p] = jnp.zeros((8, LN), BF16)
    incb[p] = jnp.zeros((8, LN), BF16)

    pl.semaphore_wait(barrier, DOM - 1 + NX - 1)

    def relay(i, carry):
        q = lax.rem(p + i, DOM)
        remote(msg.at[q], inc.at[p], r_s, r_r, q, x).start()
        return carry

    lax.fori_loop(1, DOM, relay, 0)

    frow = jnp.broadcast_to(from_ref[...], (LN, ND))
    fcol = frow.T
    fcol4 = jnp.concatenate([fcol] * 4, 1)
    for c in range(4):
        gat_i[c * ND : (c + 1) * ND, :] = onehot(
            (fcol4 - ND) * 4 + c == iota((ND, 4 * LN), 1)
        )
    stay = onehot(fcol == iota((ND, LN), 1))

    lane = iota((LN, LN), 1)
    subl = iota((LN, LN), 0)

    def selections(b, carry):
        rows = pl.ds(pl.multiple_of(b * LN, LN), LN)
        srow = jnp.broadcast_to(snd_ref[pl.ds(b, 1), :], (LN, LN))
        rrow = jnp.broadcast_to(rcv_ref[pl.ds(b, 1), :], (LN, LN))
        scol = srow.T
        rcol = rrow.T
        for k in range(TR // LN):
            sel_s[rows, k * LN : (k + 1) * LN] = onehot(scol == lane + k * LN)
            sel_st[k * LN : (k + 1) * LN, rows] = onehot(srow == subl + k * LN)
        r = onehot(rcol == lane)
        sel_r[rows, :LN] = r
        sel_r[rows, LN:] = r
        sel_rt[:, rows] = onehot(rrow == subl)
        return carry

    lax.fori_loop(0, ED // LN, selections, 0)
    table[pl.ds(NX * ND + 32, TR - NX * ND - 32), :] = jnp.zeros((TR - NX * ND - 32, H), BF16)

    loads[0].wait()
    loads[1].wait()

    def edge_term(b, carry):
        rows = pl.ds(pl.multiple_of(b * EB, EB), EB)
        pre[rows, :] = dot(e[rows, :], ein[:H, :])
        return carry

    lax.fori_loop(0, ED // EB, edge_term, 0)

    pltpu.make_async_copy(inc.at[pl.ds(0, DOM - 1)], inc.at[pl.ds(0, DOM - 1)], r_r).wait()
    got = inc[...].astype(F32).reshape(4 * LN, LN).astype(BF16)
    slots = dot(gat_i[...], got)
    latent = jnp.concatenate(
        [
            (
                dot(stay, tile_ref[:, c * LN : (c + 1) * LN])
                + slots[c * ND : (c + 1) * ND, :]
            ).astype(BF16)
            for c in range(4)
        ],
        1,
    )
    lat[...] = latent
    own_rows = pl.ds(pl.multiple_of(x * ND, ND), ND)
    table[own_rows, :] = latent

    gathers = [
        remote(table.at[own_rows], table.at[own_rows], a_s.at[j], a_r.at[j], p, xpeer(j))
        for j in (1, 3, 2)
    ]
    for c in gathers:
        c.start()
    cutb = jnp.broadcast_to(cut_ref[...], (LN, 32)).astype(F32).astype(BF16)
    eye = onehot(iota((32, 32), 0) == iota((32, 32), 1))
    ccol = dot_nt(eye, cutb)
    halo_s[...] = dot(onehot(ccol == iota((32, LN), 1).astype(F32)), latent).astype(BF16)
    halos = [
        remote(halo_s.at[pl.ds(16, 16)], table.at[pl.ds(512, 16)], a_s.at[0], a_r.at[0], up, x),
        remote(halo_s.at[pl.ds(0, 16)], table.at[pl.ds(528, 16)], a_s.at[4], a_r.at[4], dn, x),
    ]
    for c in halos:
        c.start()

    rh, rl = hi_lo(dot(latent, ein[2 * H :, :]))
    recv_proj = jnp.concatenate([rh, rl], 0)

    def recv_term(b, carry):
        rows = pl.ds(pl.multiple_of(b * EB, EB), EB)
        pre[rows, :] += dot(sel_r[rows, :], recv_proj)
        return carry

    lax.fori_loop(0, ED // EB, recv_term, 0)
    prow = dot_nt(pickb, quad)
    pq = iota((ND, 4 * LN), 1) % 4
    pn = iota((ND, 4 * LN), 0).astype(F32)
    frow4 = jnp.broadcast_to(from_ref[...], (4 * LN, ND))
    fq = iota((4 * LN, ND), 0)
    for c in range(4):
        back_o[c * ND : (c + 1) * ND, :] = onehot((prow == pn) & (pq == c))
        back_p[:, c * ND : (c + 1) * ND] = onehot((frow4 - ND) * 4 + c == fq)
    for c in loads[2:]:
        c.wait()

    for c in gathers:
        c.wait_recv()
    for c in halos:
        c.wait_recv()

    def edge_forward(b, carry):
        rows = pl.ds(pl.multiple_of(b * EB, EB), EB)
        send_rows = dot(sel_s[rows, :], table[...]).astype(BF16)
        a, da = silu_pair(pre[rows, :] + dot(send_rows, ein[H : 2 * H, :]))
        a = a.astype(BF16)
        act[rows, :] = a
        dsilu[rows, :] = da
        yn, inv = norm(dot(a, eout[...]))
        normed[rows, :] = yn
        einv[rows, :] = jnp.broadcast_to(inv, (EB, LN))
        enew[rows, :] = (e[rows, :].astype(F32) + yn).astype(BF16)
        return carry

    lax.fori_loop(0, ED // EB, edge_forward, 0)
    st_new = pltpu.make_async_copy(enew, edgeup_hbm, lsem.at[6])
    st_new.start()

    agg = dot(sel_rt[...], enew[...]).astype(BF16)
    node_act, node_dsilu = silu_pair(dot(latent, nin[:H, :]) + dot(agg, nin[H:, :]))
    node_act = node_act.astype(BF16)
    nnorm, ninv = norm(dot(node_act, nout[...]))
    nodeup_ref[...] = (latent.astype(F32) + nnorm).astype(BF16)
    ncot = ncot_ref[...].astype(F32)
    nlg = norm_grad(nnorm, ninv, ncot).astype(BF16)
    npg = (dot_nt(nlg, nout[...]) * node_dsilu).astype(BF16)
    agh, agl = hi_lo(dot_nt(npg, nin[H:, :]))
    agg_grad = jnp.concatenate([agh, agl], 0)
    node_direct = ncot + dot_nt(npg, nin[:H, :])
    wg[4 * H : 5 * H, :] = dot_tn(latent, npg)
    wg[5 * H : 6 * H, :] = dot_tn(agg, npg)
    wg[6 * H :, :] = dot_tn(node_act, nlg)

    half = 7 * ED // 12

    def two_blocks(block, k, side):
        base = 2 * half * block + 4 * 56 * k + 56 * side
        return jnp.concatenate(
            [
                wg[pl.ds(pl.multiple_of(base, 8), 56), :],
                wg[pl.ds(pl.multiple_of(base + 112, 8), 56), :],
            ],
            0,
        )

    def core_copy(block):
        rows = pl.ds(half * block, half)
        return remote(
            csend.at[rows], crecv.at[rows], c_s.at[block], c_r.at[block], sib, x
        )

    def pack_core(block):
        def body(k, carry):
            rows = pl.ds(pl.multiple_of(half * block + 112 * k, 16), 112)
            csend[rows, :] = two_blocks(block, k, 1 - core).astype(BF16)
            return carry

        lax.fori_loop(0, 4, body, 0)
        core_copy(block).start()

    def x_copy(block, j):
        t = xpeer(j)
        cols = pl.ds(pl.multiple_of(t * LN, LN), LN)
        i = 3 * block + j - 1
        return remote(
            chip.at[pl.ds(half * block, half), cols], rx.at[i], s2_s.at[i], s2_r.at[i], p, t
        )

    def y_index(block):
        return lax.rem(block - y + NY, NY)

    def y_copy(src, dst, ss, rs, block):
        j = y_index(block) - 1
        return remote(src, dst.at[j], ss.at[j], rs.at[j], p + (block - y) * NC * NZ, x)

    def y1_copy(block):
        return y_copy(chip.at[pl.ds(half * block, half)], ry1, s3_s, s3_r, block)

    def y0_copy(block):
        return y_copy(bx.at[block], ry, s3_s, s3_r, block)

    def x1_copy(j):
        t = xpeer(j)
        cols = pl.ds(pl.multiple_of(t * LN, LN), LN)
        return remote(b1.at[:, cols], rx1.at[j - 1], s2_s.at[j - 1], s2_r.at[j - 1], p, t)

    def combine(block):
        core_copy(block).wait_recv()

        def body(k, carry):
            rows = pl.ds(pl.multiple_of(half * block + 112 * k, 16), 112)
            chip[rows, :] = (
                two_blocks(block, k, core) + crecv[rows, :].astype(F32)
            ).astype(BF16)
            return carry

        lax.fori_loop(0, 4, body, 0)

        @pl.when(core == 0)
        def _():
            for j in (1, 3, 2):
                x_copy(block, j).start()

        @pl.when((core == 1) & (y != block))
        def _():
            y1_copy(block).start()

    pack_core(3)

    def edge_backward(b, carry):
        rows = pl.ds(pl.multiple_of(b * EB, EB), EB)
        upst = cot[rows, :].astype(F32) + dot(sel_r[rows, :], agg_grad)
        g = norm_grad(normed[rows, :], einv[rows, :1], upst).astype(BF16)
        plg[rows, :] = g
        pg = (dot_nt(g, eout[...]) * dsilu[rows, :]).astype(BF16)
        ppg[rows, :] = pg
        egrad[rows, :] = (upst + dot_nt(pg, ein[:H, :])).astype(BF16)
        return carry

    lax.fori_loop(0, ED // EB, edge_backward, 0)
    gsum[...] = dot(sel_st[...], ppg[...])
    gs[...] = gsum[...].astype(BF16)

    def own_of(t):
        return pl.ds(pl.multiple_of(t * ND, ND), ND)

    scatters = [
        remote(gs.at[own_of(xpeer(j))], gr.at[j - 1], g_s.at[j], g_r.at[j], p, xpeer(j))
        for j in (1, 3, 2)
    ] + [
        remote(gs.at[pl.ds(512, 16)], hb.at[pl.ds(16, 16)], g_s.at[0], g_r.at[0], dn, x),
        remote(gs.at[pl.ds(528, 16)], hb.at[pl.ds(0, 16)], g_s.at[4], g_r.at[4], up, x),
    ]
    for c in scatters:
        c.start()
    st_grad = pltpu.make_async_copy(egrad, edgegrad_hbm, lsem.at[7])
    st_grad.start()
    combine(3)
    wg[3 * H : 4 * H, :] = dot_tn(act[...], plg[...])
    pack_core(2)
    grecv = dot(sel_rt[...], ppg[...]).astype(BF16)
    node_part = node_direct + dot_nt(grecv, ein[2 * H :, :])
    wg[2 * H : 3 * H, :] = dot_tn(latent, grecv)
    wg[H : 2 * H, :] = dot_tn(table[...], gs[...])
    pack_core(1)
    combine(2)
    wg[:H, :] = dot_tn(e[...], ppg[...])
    pack_core(0)
    combine(1)

    for c in scatters:
        c.wait_recv()
    crow = jnp.broadcast_to(cut_ref[...], (ND, 32))
    total = dot(onehot(crow == iota((ND, 32), 0)), hb[...])
    total += gsum[own_rows, :]
    for j in range(3):
        total += gr[j].astype(F32)
    node_grad = (node_part + dot_nt(total.astype(BF16), ein[H : 2 * H, :])).astype(BF16)
    ng = jnp.concatenate([node_grad[:, c * LN : (c + 1) * LN] for c in range(4)], 0)
    msgb[...] = dot(back_p[...], ng).reshape(DOM, 8, LN).astype(BF16)

    def relay_back(i, carry):
        q = lax.rem(p + i, DOM)
        remote(msgb.at[q], incb.at[p], rb_s, rb_r, q, x).start()
        return carry

    lax.fori_loop(1, DOM, relay_back, 0)
    combine(0)

    mine = pl.ds(pl.multiple_of(x * LN, LN), LN)

    @pl.when(core == 0)
    def _():
        for block in (3, 2, 1, 0):
            total = chip[pl.ds(half * block, half), mine].astype(F32)
            for j in (1, 3, 2):
                x_copy(block, j).wait_recv()
                total += rx[3 * block + j - 1].astype(F32)
            bx[block] = total.astype(BF16)

            @pl.when(y != block)
            def _():
                y0_copy(block).start()

        total = bx[y].astype(F32)
        for j in range(3):
            y0_copy(lax.rem(y + j + 1, NY)).wait_recv()
            total += ry[j].astype(F32)
        zown[...] = total

    @pl.when(core == 1)
    def _():
        total = chip[pl.ds(pl.multiple_of(half * y, 16), half), :].astype(F32)
        for j in range(3):
            y1_copy(lax.rem(y + j + 1, NY)).wait_recv()
            total += ry1[j].astype(F32)
        b1[...] = total.astype(BF16)
        for j in (1, 3, 2):
            x1_copy(j).start()
        total = b1[:, mine].astype(F32)
        for j in (1, 3, 2):
            x1_copy(j).wait_recv()
            total += rx1[j - 1].astype(F32)
        zown[...] = total

    for k in range(NZ):
        zp[k] = jnp.concatenate(
            [zown[56 * k : 56 * k + 56, :], jnp.zeros((8, LN), F32)], 0
        ).astype(BF16)

    def z_copy(j):
        zz = lax.rem(z + j, NZ)
        return remote(
            zp.at[zz], rz.at[j - 1], z_s.at[j - 1], z_r.at[j - 1], p + (zz - z) * NC, x
        )

    for j in range(1, NZ):
        z_copy(j).start()

    pltpu.make_async_copy(incb.at[pl.ds(0, DOM - 1)], incb.at[pl.ds(0, DOM - 1)], rb_r).wait()
    back = incb[...].astype(F32).reshape(4 * LN, LN).astype(BF16)
    slots = dot(back_o[...], back)
    stay_t = onehot(frow == iota((LN, ND), 0))
    latgrad_ref[...] = jnp.concatenate(
        [
            (
                dot(stay_t, node_grad[:, c * LN : (c + 1) * LN])
                + slots[c * ND : (c + 1) * ND, :]
            ).astype(BF16)
            for c in range(4)
        ],
        1,
    )

    total = zown[pl.ds(pl.multiple_of(56 * z, 8), 56), :]
    for j in range(1, NZ):
        z_copy(j).wait_recv()
        total += rz[j - 1].astype(F32)[:56, :]
    wgrad_ref[...] = total

    pltpu.make_async_copy(msg.at[pl.ds(0, DOM - 1)], msg.at[pl.ds(0, DOM - 1)], r_s).wait()
    pltpu.make_async_copy(msgb.at[pl.ds(0, DOM - 1)], msgb.at[pl.ds(0, DOM - 1)], rb_s).wait()
    for c in gathers + halos + scatters:
        c.wait_send()
    for block in range(4):
        core_copy(block).wait_send()

    @pl.when(core == 0)
    def _():
        for block in range(4):
            for j in (1, 3, 2):
                x_copy(block, j).wait_send()
        for j in range(3):
            y0_copy(lax.rem(y + j + 1, NY)).wait_send()

    @pl.when(core == 1)
    def _():
        for j in range(3):
            y1_copy(lax.rem(y + j + 1, NY)).wait_send()
        for j in (1, 3, 2):
            x1_copy(j).wait_send()

    for j in range(1, NZ):
        z_copy(j).wait_send()
    st_new.wait()
    st_grad.wait()


def body(
    tile_latent, relay_pick, relay_from, cut_pick, edge_latent, edge_sender, edge_receiver,
    edge_in, edge_out, node_in, node_out, node_cot, edge_cot,
):
    vmem = pl.BlockSpec(memory_space=pltpu.VMEM)
    hbm = pl.BlockSpec(memory_space=pl.ANY)
    dma = pltpu.SemaphoreType.DMA
    V = pltpu.VMEM
    half = 7 * ED // 12
    scratch = [
        V((ED, H), BF16), V((ED, H), BF16), V((3 * H, H), BF16), V((H, H), BF16),
        V((2 * H, H), BF16), V((H, H), BF16), dma((8,)),
        V((DOM, 8, LN), BF16), V((DOM, 8, LN), BF16), V((DOM, 8, LN), BF16), V((DOM, 8, LN), BF16),
        V((TR, H), BF16), V((ND, H), BF16), V((32, H), BF16),
        V((ED, TR), BF16), V((TR, ED), BF16), V((ED, 2 * LN), BF16), V((ND, ED), BF16),
        V((4 * ND, 4 * LN), BF16), V((4 * ND, 4 * LN), BF16), V((4 * LN, 4 * ND), BF16),
        V((ED, H), F32), V((ED, H), BF16), V((ED, H), F32), V((ED, H), F32), V((ED, LN), F32),
        V((ED, H), BF16), V((ED, H), BF16), V((ED, H), BF16), V((ED, H), BF16),
        V((TR, H), F32), V((TR, H), BF16), V((3, ND, H), BF16), V((32, H), BF16), V((7 * H, H), F32),
        V((4 * half, H), BF16), V((4 * half, H), BF16), V((4 * half, H), BF16),
        V((12, half, LN), BF16), V((4, half, LN), BF16), V((3, half, LN), BF16),
        V((3, half, H), BF16), V((half, H), BF16), V((3, half, LN), BF16),
        V((half, LN), F32), V((NZ, 64, LN), BF16), V((NZ - 1, 64, LN), BF16),
        dma, dma, dma((5,)), dma((5,)), dma, dma, dma((5,)), dma((5,)), dma((4,)), dma((4,)),
        dma((12,)), dma((12,)), dma((3,)), dma((3,)), dma((NZ - 1,)), dma((NZ - 1,)),
    ]
    return pl.pallas_call(
        kernel,
        out_shape=(
            jax.ShapeDtypeStruct((ND, H), BF16),
            jax.ShapeDtypeStruct((ED, H), BF16),
            jax.ShapeDtypeStruct((ND, H), BF16),
            jax.ShapeDtypeStruct((ED, H), BF16),
            jax.ShapeDtypeStruct((56, LN), F32),
        ),
        in_specs=[vmem] * 7 + [hbm] * 6,
        out_specs=(vmem, hbm, vmem, hbm, vmem),
        scratch_shapes=scratch,
        compiler_params=pltpu.CompilerParams(
            collective_id=0, has_side_effects=True, vmem_limit_bytes=56 * 2**20
        ),
    )(
        tile_latent, relay_pick, relay_from.reshape(1, ND), cut_pick,
        edge_sender.reshape(ED // LN, LN), edge_receiver.reshape(ED // LN, LN), node_cot,
        edge_latent, edge_cot, edge_in, edge_out, node_in, node_out,
    )


def solution(mesh):
    rows = P(("dom", "tile"), None)
    flat = P(("dom", "tile"))
    in_specs = (
        rows, rows, flat, rows, rows, flat, flat, P(), P(), P(), P(), rows, rows,
    )
    out_specs = (rows, rows, rows, rows, P("dom", "tile"))
    return jax.shard_map(body, mesh=mesh, in_specs=in_specs, out_specs=out_specs, check_vma=False)
```

```python
import jax
import jax.numpy as jnp
from jax import lax
from jax.experimental import pallas as pl
from jax.experimental.pallas import tpu as pltpu
from jax.sharding import PartitionSpec as P

EPSILON = 1e-05
MESH = pl.DeviceIdType.MESH
F32 = jnp.float32
BF16 = jnp.bfloat16
NX, NY, NZ, NC = 4, 4, 8, 2
DOM = NY * NZ * NC
H = 512
ND = 128
ED = 768
EB = 256
TR = 640
LN = 128
SUB = 224
RX = 112
RY = SUB - RX


def iota(shape, dim):
    return lax.broadcasted_iota(jnp.int32, shape, dim)


def onehot(mask):
    return jnp.where(mask, 1.0, 0.0).astype(BF16)


def dot(a, b):
    return lax.dot_general(a, b, (((1,), (0,)), ((), ())), preferred_element_type=F32)


def dot_nt(a, b):
    return lax.dot_general(a, b, (((1,), (1,)), ((), ())), preferred_element_type=F32)


def dot_tn(a, b):
    return lax.dot_general(a, b, (((0,), (0,)), ((), ())), preferred_element_type=F32)


def norm(v):
    center = v - jnp.mean(v, -1, keepdims=True)
    inv = lax.rsqrt(jnp.mean(center * center, -1, keepdims=True) + EPSILON)
    return center * inv, inv


def norm_grad(normed, inv, up):
    mean_up = jnp.mean(up, -1, keepdims=True)
    mean_cross = jnp.mean(up * normed, -1, keepdims=True)
    return inv * (up - mean_up - normed * mean_cross)


def silu_pair(v):
    sig = 1.0 / (1.0 + jnp.exp(-v))
    act = v * sig
    return act, sig + act * (1.0 - sig)


def hi_lo(v):
    hi = v.astype(BF16)
    return hi, (v - hi.astype(F32)).astype(BF16)


def kernel(
    tile_ref, pick_ref, from_ref, cut_ref, snd_ref, rcv_ref, ncot_ref,
    e_hbm, cot_hbm, ein_hbm, eout_hbm, nin_hbm, nout_hbm,
    nodeup_ref, edgeup_hbm, latgrad_ref, edgegrad_hbm, wgrad_ref,
    e, cot, ein, eout, nin, nout, lsem,
    msg, inc, msgb, incb, table, lat, halo_s,
    sel_s, sel_st, sel_r, sel_rt, gat_i, back_o, back_p,
    pre, act, dsilu, normed, einv, enew, egrad, plg, ppg,
    gsum, gs, gr, hb, wg,
    csend, crecv, chip, rx, bx, ry, ry1, b1, rx2, zown, zp, rz,
    r_s, r_r, a_s, a_r, rb_s, rb_r, g_s, g_r, c_s, c_r,
    x1_s, x1_r, y1_s, y1_r, y2_s, y2_r, x2_s, x2_r, z_s, z_r,
):
    p = lax.axis_index("dom")
    x = lax.axis_index("tile")
    core = lax.rem(p, NC)
    z = lax.rem(p // NC, NZ)
    y = p // (NC * NZ)
    up = lax.rem(p + 1, DOM)
    dn = lax.rem(p + DOM - 1, DOM)
    sib = p + 1 - 2 * core

    def xpeer(j):
        return lax.rem(x + j, NX)

    def remote(src, dst, ss, rs, d, t):
        return pltpu.make_async_remote_copy(
            src, dst, ss, rs, device_id=(d, t), device_id_type=MESH
        )

    barrier = pltpu.get_barrier_semaphore()

    def greet(i, carry):
        pl.semaphore_signal(
            barrier, 1, device_id=(lax.rem(p + i, DOM), x), device_id_type=MESH
        )
        return carry

    lax.fori_loop(1, DOM, greet, 0)
    for j in range(1, NX):
        pl.semaphore_signal(barrier, 1, device_id=(p, xpeer(j)), device_id_type=MESH)

    loads = [
        pltpu.make_async_copy(s, d, lsem.at[i])
        for i, (s, d) in enumerate(
            (
                (e_hbm, e), (ein_hbm, ein), (eout_hbm, eout), (nin_hbm, nin),
                (nout_hbm, nout), (cot_hbm, cot),
            )
        )
    ]
    for c in loads:
        c.start()

    pickb = jnp.broadcast_to(pick_ref[...], (ND, LN)).astype(F32).astype(BF16)
    quad = onehot(iota((4 * LN, LN), 0) // 4 == iota((4 * LN, LN), 1))
    rep = dot_nt(quad, pickb)
    qlane = iota((4 * LN, LN), 1).astype(F32)
    qmod = iota((4 * LN, LN), 0) % 4
    out = jnp.zeros((4 * LN, LN), F32)
    for c in range(4):
        out += dot(
            onehot((rep == qlane) & (qmod == c)), tile_ref[:, c * LN : (c + 1) * LN]
        )
    msg[...] = out.reshape(DOM, 8, LN).astype(BF16)
    inc[p] = jnp.zeros((8, LN), BF16)
    incb[p] = jnp.zeros((8, LN), BF16)

    pl.semaphore_wait(barrier, DOM - 1 + NX - 1)

    def relay(i, carry):
        q = lax.rem(p + i, DOM)
        remote(msg.at[q], inc.at[p], r_s, r_r, q, x).start()
        return carry

    lax.fori_loop(1, DOM, relay, 0)

    frow = jnp.broadcast_to(from_ref[...], (LN, ND))
    fcol = frow.T
    fcol4 = jnp.concatenate([fcol] * 4, 1)
    for c in range(4):
        gat_i[c * ND : (c + 1) * ND, :] = onehot(
            (fcol4 - ND) * 4 + c == iota((ND, 4 * LN), 1)
        )
    stay = onehot(fcol == iota((ND, LN), 1))

    lane = iota((LN, LN), 1)
    subl = iota((LN, LN), 0)

    def selections(b, carry):
        rows = pl.ds(pl.multiple_of(b * LN, LN), LN)
        srow = jnp.broadcast_to(snd_ref[pl.ds(b, 1), :], (LN, LN))
        rrow = jnp.broadcast_to(rcv_ref[pl.ds(b, 1), :], (LN, LN))
        scol = srow.T
        rcol = rrow.T
        for k in range(TR // LN):
            sel_s[rows, k * LN : (k + 1) * LN] = onehot(scol == lane + k * LN)
            sel_st[k * LN : (k + 1) * LN, rows] = onehot(srow == subl + k * LN)
        r = onehot(rcol == lane)
        sel_r[rows, :LN] = r
        sel_r[rows, LN:] = r
        sel_rt[:, rows] = onehot(rrow == subl)
        return carry

    lax.fori_loop(0, ED // LN, selections, 0)
    table[pl.ds(NX * ND + 32, TR - NX * ND - 32), :] = jnp.zeros((TR - NX * ND - 32, H), BF16)

    loads[0].wait()
    loads[1].wait()

    def edge_term(b, carry):
        rows = pl.ds(pl.multiple_of(b * EB, EB), EB)
        pre[rows, :] = dot(e[rows, :], ein[:H, :])
        return carry

    lax.fori_loop(0, ED // EB, edge_term, 0)

    pltpu.make_async_copy(inc.at[pl.ds(0, DOM - 1)], inc.at[pl.ds(0, DOM - 1)], r_r).wait()
    got = inc[...].astype(F32).reshape(4 * LN, LN).astype(BF16)
    slots = dot(gat_i[...], got)
    latent = jnp.concatenate(
        [
            (
                dot(stay, tile_ref[:, c * LN : (c + 1) * LN])
                + slots[c * ND : (c + 1) * ND, :]
            ).astype(BF16)
            for c in range(4)
        ],
        1,
    )
    lat[...] = latent
    own_rows = pl.ds(pl.multiple_of(x * ND, ND), ND)
    table[own_rows, :] = latent

    gathers = [
        remote(table.at[own_rows], table.at[own_rows], a_s.at[j], a_r.at[j], p, xpeer(j))
        for j in (1, 3, 2)
    ]
    for c in gathers:
        c.start()
    cutb = jnp.broadcast_to(cut_ref[...], (LN, 32)).astype(F32).astype(BF16)
    eye = onehot(iota((32, 32), 0) == iota((32, 32), 1))
    ccol = dot_nt(eye, cutb)
    halo_s[...] = dot(onehot(ccol == iota((32, LN), 1).astype(F32)), latent).astype(BF16)
    halos = [
        remote(halo_s.at[pl.ds(16, 16)], table.at[pl.ds(512, 16)], a_s.at[0], a_r.at[0], up, x),
        remote(halo_s.at[pl.ds(0, 16)], table.at[pl.ds(528, 16)], a_s.at[4], a_r.at[4], dn, x),
    ]
    for c in halos:
        c.start()

    rh, rl = hi_lo(dot(latent, ein[2 * H :, :]))
    recv_proj = jnp.concatenate([rh, rl], 0)

    def recv_term(b, carry):
        rows = pl.ds(pl.multiple_of(b * EB, EB), EB)
        pre[rows, :] += dot(sel_r[rows, :], recv_proj)
        return carry

    lax.fori_loop(0, ED // EB, recv_term, 0)
    prow = dot_nt(pickb, quad)
    pq = iota((ND, 4 * LN), 1) % 4
    pn = iota((ND, 4 * LN), 0).astype(F32)
    frow4 = jnp.broadcast_to(from_ref[...], (4 * LN, ND))
    fq = iota((4 * LN, ND), 0)
    for c in range(4):
        back_o[c * ND : (c + 1) * ND, :] = onehot((prow == pn) & (pq == c))
        back_p[:, c * ND : (c + 1) * ND] = onehot((frow4 - ND) * 4 + c == fq)
    for c in loads[2:]:
        c.wait()

    for c in gathers:
        c.wait_recv()
    for c in halos:
        c.wait_recv()

    def edge_forward(b, carry):
        rows = pl.ds(pl.multiple_of(b * EB, EB), EB)
        send_rows = dot(sel_s[rows, :], table[...]).astype(BF16)
        a, da = silu_pair(pre[rows, :] + dot(send_rows, ein[H : 2 * H, :]))
        a = a.astype(BF16)
        act[rows, :] = a
        dsilu[rows, :] = da
        yn, inv = norm(dot(a, eout[...]))
        normed[rows, :] = yn
        einv[rows, :] = jnp.broadcast_to(inv, (EB, LN))
        enew[rows, :] = (e[rows, :].astype(F32) + yn).astype(BF16)
        return carry

    lax.fori_loop(0, ED // EB, edge_forward, 0)
    st_new = pltpu.make_async_copy(enew, edgeup_hbm, lsem.at[6])
    st_new.start()

    agg = dot(sel_rt[...], enew[...]).astype(BF16)
    node_act, node_dsilu = silu_pair(dot(latent, nin[:H, :]) + dot(agg, nin[H:, :]))
    node_act = node_act.astype(BF16)
    nnorm, ninv = norm(dot(node_act, nout[...]))
    nodeup_ref[...] = (latent.astype(F32) + nnorm).astype(BF16)
    ncot = ncot_ref[...].astype(F32)
    nlg = norm_grad(nnorm, ninv, ncot).astype(BF16)
    npg = (dot_nt(nlg, nout[...]) * node_dsilu).astype(BF16)
    agh, agl = hi_lo(dot_nt(npg, nin[H:, :]))
    agg_grad = jnp.concatenate([agh, agl], 0)
    node_direct = ncot + dot_nt(npg, nin[:H, :])
    wg[4 * H : 5 * H, :] = dot_tn(latent, npg)
    wg[5 * H : 6 * H, :] = dot_tn(agg, npg)
    wg[6 * H :, :] = dot_tn(node_act, nlg)

    def two_blocks(block, k, side):
        base = 2 * SUB * block + 4 * 56 * k + 56 * side
        return jnp.concatenate(
            [
                wg[pl.ds(pl.multiple_of(base, 8), 56), :],
                wg[pl.ds(pl.multiple_of(base + 112, 8), 56), :],
            ],
            0,
        )

    def core_copy(block):
        rows = pl.ds(SUB * block, SUB)
        return remote(
            csend.at[rows], crecv.at[rows], c_s.at[block], c_r.at[block], sib, x
        )

    def pack_core(block):
        for k in range(2):
            rows = pl.ds(SUB * block + 112 * k, 112)
            csend[rows, :] = two_blocks(block, k, 1 - core).astype(BF16)
        core_copy(block).start()

    def columns(t):
        return pl.ds(pl.multiple_of(t * LN, LN), LN)

    def x1_copy(block, j):
        t = xpeer(j)
        i = 3 * block + j - 1
        return remote(
            chip.at[pl.ds(SUB * block, RX), columns(t)], rx.at[i], x1_s.at[i], x1_r.at[i], p, t
        )

    def y_copy(src, dst, ss, rs, block):
        i = 2 * (lax.rem(block // 2 - y + NY, NY) - 1) + block % 2
        return remote(
            src, dst.at[i], ss.at[i], rs.at[i], p + (block // 2 - y) * NC * NZ, x
        )

    def y1_copy(block):
        return y_copy(chip.at[pl.ds(SUB * block + RX, RY)], ry1, y1_s, y1_r, block)

    def y2_copy(block):
        return y_copy(bx.at[block], ry, y2_s, y2_r, block)

    def x2_copy(s, j):
        t = xpeer(j)
        i = 3 * s + j - 1
        return remote(b1.at[s, :, columns(t)], rx2.at[i], x2_s.at[i], x2_r.at[i], p, t)

    def y_block(j, s):
        return 2 * lax.rem(y + j, NY) + s

    def combine(block):
        core_copy(block).wait_recv()
        for k in range(2):
            rows = pl.ds(SUB * block + 112 * k, 112)
            chip[rows, :] = (
                two_blocks(block, k, core) + crecv[rows, :].astype(F32)
            ).astype(BF16)

        @pl.when(y != block // 2)
        def _():
            y1_copy(block).start()

        for j in (1, 3, 2):
            x1_copy(block, j).start()

    mine = columns(x)

    def finish_x(block):
        total = chip[pl.ds(SUB * block, RX), mine].astype(F32)
        for j in (1, 3, 2):
            x1_copy(block, j).wait_recv()
            total += rx[3 * block + j - 1].astype(F32)
        bx[block] = total.astype(BF16)

        @pl.when(y != block // 2)
        def _():
            y2_copy(block).start()

    def finish_y(s):
        own = pl.ds(pl.multiple_of(SUB * (2 * y + s) + RX, 16), RY)
        total = chip[own, :].astype(F32)
        for j in range(1, NY):
            y1_copy(y_block(j, s)).wait_recv()
            total += ry1[2 * (j - 1) + s].astype(F32)
        b1[s] = total.astype(BF16)
        for j in (1, 3, 2):
            x2_copy(s, j).start()

    for block in (7, 6, 5):
        pack_core(block)

    def edge_backward(b, carry):
        rows = pl.ds(pl.multiple_of(b * EB, EB), EB)
        upst = cot[rows, :].astype(F32) + dot(sel_r[rows, :], agg_grad)
        g = norm_grad(normed[rows, :], einv[rows, :1], upst).astype(BF16)
        plg[rows, :] = g
        pg = (dot_nt(g, eout[...]) * dsilu[rows, :]).astype(BF16)
        ppg[rows, :] = pg
        egrad[rows, :] = (upst + dot_nt(pg, ein[:H, :])).astype(BF16)
        return carry

    lax.fori_loop(0, 1, edge_backward, 0)
    for block in (7, 6, 5):
        combine(block)
    lax.fori_loop(1, ED // EB, edge_backward, 0)
    gsum[...] = dot(sel_st[...], ppg[...])
    gs[...] = gsum[...].astype(BF16)

    def own_of(t):
        return pl.ds(pl.multiple_of(t * ND, ND), ND)

    scatters = [
        remote(gs.at[own_of(xpeer(j))], gr.at[j - 1], g_s.at[j], g_r.at[j], p, xpeer(j))
        for j in (1, 3, 2)
    ] + [
        remote(gs.at[pl.ds(512, 16)], hb.at[pl.ds(16, 16)], g_s.at[0], g_r.at[0], dn, x),
        remote(gs.at[pl.ds(528, 16)], hb.at[pl.ds(0, 16)], g_s.at[4], g_r.at[4], up, x),
    ]
    for c in scatters:
        c.start()
    st_grad = pltpu.make_async_copy(egrad, edgegrad_hbm, lsem.at[7])
    st_grad.start()
    wg[3 * H : 4 * H, :] = dot_tn(act[...], plg[...])
    grecv = dot(sel_rt[...], ppg[...]).astype(BF16)
    wg[2 * H : 3 * H, :] = dot_tn(latent, grecv)
    pack_core(3)
    wg[H : 2 * H, :] = dot_tn(table[...], gs[...])
    wg[:H, :] = dot_tn(e[...], ppg[...])
    for block in (1, 2, 0, 4):
        pack_core(block)
    node_part = node_direct + dot_nt(grecv, ein[2 * H :, :])
    for block in (3, 1, 2, 0, 4):
        combine(block)
    for block in (7, 6, 5):
        finish_x(block)

    for c in scatters:
        c.wait_recv()
    crow = jnp.broadcast_to(cut_ref[...], (ND, 32))
    total = dot(onehot(crow == iota((ND, 32), 0)), hb[...])
    total += gsum[own_rows, :]
    for j in range(3):
        total += gr[j].astype(F32)
    node_grad = (node_part + dot_nt(total.astype(BF16), ein[H : 2 * H, :])).astype(BF16)
    ng = jnp.concatenate([node_grad[:, c * LN : (c + 1) * LN] for c in range(4)], 0)
    msgb[...] = dot(back_p[...], ng).reshape(DOM, 8, LN).astype(BF16)

    def relay_back(i, carry):
        q = lax.rem(p + i, DOM)
        remote(msgb.at[q], incb.at[p], rb_s, rb_r, q, x).start()
        return carry

    lax.fori_loop(1, DOM, relay_back, 0)

    def z_copy(t):
        i = lax.rem(t - z + NZ, NZ) - 1
        return remote(zp.at[t], rz.at[i], z_s.at[i], z_r.at[i], p + (t - z) * NC, x)

    def half_sum(s):
        part = bx[2 * y + s].astype(F32)
        for j in range(1, NY):
            y2_copy(y_block(j, s)).wait_recv()
            part += ry[2 * (j - 1) + s].astype(F32)
        rest = b1[s, :, mine].astype(F32)
        for j in (1, 3, 2):
            x2_copy(s, j).wait_recv()
            rest += rx2[3 * s + j - 1].astype(F32)
        total = jnp.concatenate([part, rest], 0)
        zown[SUB * s : SUB * (s + 1), :] = total
        for k in range(4):
            zp[4 * s + k] = jnp.concatenate(
                [total[56 * k : 56 * k + 56, :], jnp.zeros((8, LN), F32)], 0
            ).astype(BF16)
        for k in range(4):
            t = 4 * s + k

            @pl.when(t != z)
            def _():
                z_copy(t).start()

    for block in (3, 1):
        finish_x(block)
    finish_y(1)
    for block in (4, 2, 0):
        finish_x(block)
    finish_y(0)
    half_sum(1)
    half_sum(0)

    pltpu.make_async_copy(incb.at[pl.ds(0, DOM - 1)], incb.at[pl.ds(0, DOM - 1)], rb_r).wait()
    back = incb[...].astype(F32).reshape(4 * LN, LN).astype(BF16)
    slots = dot(back_o[...], back)
    stay_t = onehot(frow == iota((LN, ND), 0))
    latgrad_ref[...] = jnp.concatenate(
        [
            (
                dot(stay_t, node_grad[:, c * LN : (c + 1) * LN])
                + slots[c * ND : (c + 1) * ND, :]
            ).astype(BF16)
            for c in range(4)
        ],
        1,
    )

    total = zown[pl.ds(pl.multiple_of(56 * z, 8), 56), :]
    for j in range(1, NZ):
        z_copy(lax.rem(z + j, NZ)).wait_recv()
        total += rz[j - 1].astype(F32)[:56, :]
    wgrad_ref[...] = total

    pltpu.make_async_copy(msg.at[pl.ds(0, DOM - 1)], msg.at[pl.ds(0, DOM - 1)], r_s).wait()
    pltpu.make_async_copy(msgb.at[pl.ds(0, DOM - 1)], msgb.at[pl.ds(0, DOM - 1)], rb_s).wait()
    for c in gathers + halos + scatters:
        c.wait_send()
    for block in range(8):
        core_copy(block).wait_send()
        for j in (1, 3, 2):
            x1_copy(block, j).wait_send()
    for s in range(2):
        for j in range(1, NY):
            y1_copy(y_block(j, s)).wait_send()
            y2_copy(y_block(j, s)).wait_send()
            x2_copy(s, j).wait_send()
    for j in range(1, NZ):
        z_copy(lax.rem(z + j, NZ)).wait_send()
    st_new.wait()
    st_grad.wait()


def hand_over(*refs):
    for a, b in zip(refs[:5], refs[5:]):
        b[...] = a[...]


def body(
    tile_latent, relay_pick, relay_from, cut_pick, edge_latent, edge_sender, edge_receiver,
    edge_in, edge_out, node_in, node_out, node_cot, edge_cot,
):
    vmem = pl.BlockSpec(memory_space=pltpu.VMEM)
    hbm = pl.BlockSpec(memory_space=pl.ANY)
    dma = pltpu.SemaphoreType.DMA
    V = pltpu.VMEM
    scratch = [
        V((ED, H), BF16), V((ED, H), BF16), V((3 * H, H), BF16), V((H, H), BF16),
        V((2 * H, H), BF16), V((H, H), BF16), dma((8,)),
        V((DOM, 8, LN), BF16), V((DOM, 8, LN), BF16), V((DOM, 8, LN), BF16), V((DOM, 8, LN), BF16),
        V((TR, H), BF16), V((ND, H), BF16), V((32, H), BF16),
        V((ED, TR), BF16), V((TR, ED), BF16), V((ED, 2 * LN), BF16), V((ND, ED), BF16),
        V((4 * ND, 4 * LN), BF16), V((4 * ND, 4 * LN), BF16), V((4 * LN, 4 * ND), BF16),
        V((ED, H), F32), V((ED, H), BF16), V((ED, H), F32), V((ED, H), F32), V((ED, LN), F32),
        V((ED, H), BF16), V((ED, H), BF16), V((ED, H), BF16), V((ED, H), BF16),
        V((TR, H), F32), V((TR, H), BF16), V((3, ND, H), BF16), V((32, H), BF16), V((7 * H, H), F32),
        V((8 * SUB, H), BF16), V((8 * SUB, H), BF16), V((8 * SUB, H), BF16),
        V((24, RX, LN), BF16), V((8, RX, LN), BF16), V((6, RX, LN), BF16),
        V((6, RY, H), BF16), V((2, RY, H), BF16), V((6, RY, LN), BF16),
        V((2 * SUB, LN), F32), V((NZ, 64, LN), BF16), V((NZ - 1, 64, LN), BF16),
        dma, dma, dma((5,)), dma((5,)), dma, dma, dma((5,)), dma((5,)), dma((8,)), dma((8,)),
        dma((24,)), dma((24,)), dma((6,)), dma((6,)), dma((6,)), dma((6,)), dma((6,)), dma((6,)),
        dma((NZ - 1,)), dma((NZ - 1,)),
    ]
    shapes = (
        jax.ShapeDtypeStruct((ND, H), BF16),
        jax.ShapeDtypeStruct((ED, H), BF16),
        jax.ShapeDtypeStruct((ND, H), BF16),
        jax.ShapeDtypeStruct((ED, H), BF16),
        jax.ShapeDtypeStruct((56, LN), F32),
    )
    parts = pl.pallas_call(
        kernel,
        out_shape=shapes,
        in_specs=[vmem] * 7 + [hbm] * 6,
        out_specs=(vmem, hbm, vmem, hbm, vmem),
        scratch_shapes=scratch,
        compiler_params=pltpu.CompilerParams(
            collective_id=0, has_side_effects=True, vmem_limit_bytes=56 * 2**20
        ),
    )(
        tile_latent, relay_pick, relay_from.reshape(1, ND), cut_pick,
        edge_sender.reshape(ED // LN, LN), edge_receiver.reshape(ED // LN, LN), node_cot,
        edge_latent, edge_cot, edge_in, edge_out, node_in, node_out,
    )
    return pl.pallas_call(
        hand_over,
        out_shape=shapes,
        in_specs=[vmem] * 5,
        out_specs=(vmem,) * 5,
        compiler_params=pltpu.CompilerParams(vmem_limit_bytes=60 * 2**20),
    )(*parts)


def solution(mesh):
    rows = P(("dom", "tile"), None)
    flat = P(("dom", "tile"))
    in_specs = (
        rows, rows, flat, rows, rows, flat, flat, P(), P(), P(), P(), rows, rows,
    )
    out_specs = (rows, rows, rows, rows, P("dom", "tile"))
    return jax.shard_map(body, mesh=mesh, in_specs=in_specs, out_specs=out_specs, check_vma=False)
```

```python
import jax
import jax.numpy as jnp
from jax import lax
from jax.experimental import pallas as pl
from jax.experimental.pallas import tpu as pltpu
from jax.sharding import PartitionSpec as P

EPSILON = 1e-05
MESH = pl.DeviceIdType.MESH
F32 = jnp.float32
BF16 = jnp.bfloat16
NX, NY, NZ, NC = 4, 4, 8, 2
DOM = NY * NZ * NC
H = 512
ND = 128
ED = 768
EB = 384
EF = 768
TR = 640
LN = 128
SUB = 224
RX = 112
RY = SUB - RX


def iota(shape, dim):
    return lax.broadcasted_iota(jnp.int32, shape, dim)


def onehot(mask):
    return jnp.where(mask, 1.0, 0.0).astype(BF16)


def dot(a, b):
    return lax.dot_general(a, b, (((1,), (0,)), ((), ())), preferred_element_type=F32)


def dot_nt(a, b):
    return lax.dot_general(a, b, (((1,), (1,)), ((), ())), preferred_element_type=F32)


def dot_tn(a, b):
    return lax.dot_general(a, b, (((0,), (0,)), ((), ())), preferred_element_type=F32)


def norm(v):
    center = v - jnp.mean(v, -1, keepdims=True)
    inv = lax.rsqrt(jnp.mean(center * center, -1, keepdims=True) + EPSILON)
    return center * inv, inv


def norm_grad(normed, inv, up):
    mean_up = jnp.mean(up, -1, keepdims=True)
    mean_cross = jnp.mean(up * normed, -1, keepdims=True)
    return inv * (up - mean_up - normed * mean_cross)


def silu_pair(v):
    sig = 1.0 / (1.0 + jnp.exp(-v))
    act = v * sig
    return act, sig + act * (1.0 - sig)


def hi_lo(v):
    hi = v.astype(BF16)
    return hi, (v - hi.astype(F32)).astype(BF16)


def kernel(
    tile_ref, pick_ref, from_ref, cut_ref, snd_ref, rcv_ref, ncot_ref,
    e_hbm, cot_hbm, ein_hbm, eout_hbm, nin_hbm, nout_hbm,
    nodeup_ref, enew, latgrad_ref, egrad, wgrad_ref,
    e, cot, ein, eout, nin, nout, lsem,
    msg, inc, msgb, incb, table, lat, halo_s,
    sel_s, sel_st, sel_r, sel_rt, gat_i, back_o, back_p,
    pre, act, dsilu, normed, einv, plg, ppg,
    gsum, gs, gr, hb, wg,
    csend, crecv, chip, rx, bx, ry, ry1, b1, rx2, zown, zp, rz,
    r_s, r_r, a_s, a_r, rb_s, rb_r, g_s, g_r, c_s, c_r,
    x1_s, x1_r, y1_s, y1_r, y2_s, y2_r, x2_s, x2_r, z_s, z_r,
):
    p = lax.axis_index("dom")
    x = lax.axis_index("tile")
    core = lax.rem(p, NC)
    z = lax.rem(p // NC, NZ)
    y = p // (NC * NZ)
    up = lax.rem(p + 1, DOM)
    dn = lax.rem(p + DOM - 1, DOM)
    sib = p + 1 - 2 * core

    def xpeer(j):
        return lax.rem(x + j, NX)

    def remote(src, dst, ss, rs, d, t):
        return pltpu.make_async_remote_copy(
            src, dst, ss, rs, device_id=(d, t), device_id_type=MESH
        )

    barrier = pltpu.get_barrier_semaphore()

    def greet(i, carry):
        pl.semaphore_signal(
            barrier, 1, device_id=(lax.rem(p + i, DOM), x), device_id_type=MESH
        )
        return carry

    lax.fori_loop(1, DOM, greet, 0)
    for j in range(1, NX):
        pl.semaphore_signal(barrier, 1, device_id=(p, xpeer(j)), device_id_type=MESH)

    loads = [
        pltpu.make_async_copy(s, d, lsem.at[i])
        for i, (s, d) in enumerate(
            (
                (e_hbm, e), (ein_hbm, ein), (eout_hbm, eout), (nin_hbm, nin),
                (nout_hbm, nout), (cot_hbm, cot),
            )
        )
    ]
    for c in loads:
        c.start()

    pickb = jnp.broadcast_to(pick_ref[...], (ND, LN)).astype(F32).astype(BF16)
    quad = onehot(iota((4 * LN, LN), 0) // 4 == iota((4 * LN, LN), 1))
    rep = dot_nt(quad, pickb)
    qlane = iota((4 * LN, LN), 1).astype(F32)
    qmod = iota((4 * LN, LN), 0) % 4
    out = jnp.zeros((4 * LN, LN), F32)
    for c in range(4):
        out += dot(
            onehot((rep == qlane) & (qmod == c)), tile_ref[:, c * LN : (c + 1) * LN]
        )
    msg[...] = out.reshape(DOM, 8, LN).astype(BF16)
    inc[p] = jnp.zeros((8, LN), BF16)
    incb[p] = jnp.zeros((8, LN), BF16)

    pl.semaphore_wait(barrier, DOM - 1 + NX - 1)

    def exchange(src, dst, ss, rs):
        def step(i, last):
            dz = NZ // 2 + (i + 1) // 2 * (1 - 2 * (i % 2))
            for dy in (2, 1, 3, 0):
                for dc in (0, 1):
                    if not last or dy or dc:
                        q = lax.rem(y + dy, NY) * (NZ * NC)
                        q += lax.rem(z + dz, NZ) * NC + lax.rem(core + dc, NC)
                        remote(src.at[q], dst.at[p], ss, rs, q, x).start()

        def loop(i, carry):
            step(i, False)
            return carry

        lax.fori_loop(0, NZ - 1, loop, 0)
        step(NZ - 1, True)

    exchange(msg, inc, r_s, r_r)

    frow = jnp.broadcast_to(from_ref[...], (LN, ND))
    fcol = frow.T
    fcol4 = jnp.concatenate([fcol] * 4, 1)
    for c in range(4):
        gat_i[c * ND : (c + 1) * ND, :] = onehot(
            (fcol4 - ND) * 4 + c == iota((ND, 4 * LN), 1)
        )
    stay = onehot(fcol == iota((ND, LN), 1))

    lane = iota((LN, LN), 1)
    subl = iota((LN, LN), 0)

    def selections(b, carry):
        rows = pl.ds(pl.multiple_of(b * LN, LN), LN)
        srow = jnp.broadcast_to(snd_ref[pl.ds(b, 1), :], (LN, LN))
        rrow = jnp.broadcast_to(rcv_ref[pl.ds(b, 1), :], (LN, LN))
        scol = srow.T
        rcol = rrow.T
        for k in range(TR // LN):
            sel_s[rows, k * LN : (k + 1) * LN] = onehot(scol == lane + k * LN)
            sel_st[k * LN : (k + 1) * LN, rows] = onehot(srow == subl + k * LN)
        r = onehot(rcol == lane)
        sel_r[rows, :LN] = r
        sel_r[rows, LN:] = r
        sel_rt[:, rows] = onehot(rrow == subl)
        return carry

    lax.fori_loop(0, ED // LN, selections, 0)
    table[pl.ds(NX * ND + 32, TR - NX * ND - 32), :] = jnp.zeros((TR - NX * ND - 32, H), BF16)

    loads[0].wait()
    loads[1].wait()

    def edge_term(b, carry):
        rows = pl.ds(pl.multiple_of(b * EF, EF), EF)
        pre[rows, :] = dot(e[rows, :], ein[:H, :])
        return carry

    lax.fori_loop(0, ED // EF, edge_term, 0)

    pltpu.make_async_copy(inc.at[pl.ds(0, DOM - 1)], inc.at[pl.ds(0, DOM - 1)], r_r).wait()
    got = inc[...].astype(F32).reshape(4 * LN, LN).astype(BF16)
    slots = dot(gat_i[...], got)
    latent = jnp.concatenate(
        [
            (
                dot(stay, tile_ref[:, c * LN : (c + 1) * LN])
                + slots[c * ND : (c + 1) * ND, :]
            ).astype(BF16)
            for c in range(4)
        ],
        1,
    )
    lat[...] = latent
    own_rows = pl.ds(pl.multiple_of(x * ND, ND), ND)
    table[own_rows, :] = latent

    gathers = [
        remote(table.at[own_rows], table.at[own_rows], a_s.at[j], a_r.at[j], p, xpeer(j))
        for j in (1, 3, 2)
    ]
    for c in gathers:
        c.start()
    cutb = jnp.broadcast_to(cut_ref[...], (LN, 32)).astype(F32).astype(BF16)
    eye = onehot(iota((32, 32), 0) == iota((32, 32), 1))
    ccol = dot_nt(eye, cutb)
    halo_s[...] = dot(onehot(ccol == iota((32, LN), 1).astype(F32)), latent).astype(BF16)
    halos = [
        remote(halo_s.at[pl.ds(16, 16)], table.at[pl.ds(512, 16)], a_s.at[0], a_r.at[0], up, x),
        remote(halo_s.at[pl.ds(0, 16)], table.at[pl.ds(528, 16)], a_s.at[4], a_r.at[4], dn, x),
    ]
    for c in halos:
        c.start()

    rh, rl = hi_lo(dot(latent, ein[2 * H :, :]))
    recv_proj = jnp.concatenate([rh, rl], 0)

    def recv_term(b, carry):
        rows = pl.ds(pl.multiple_of(b * EF, EF), EF)
        pre[rows, :] += dot(sel_r[rows, :], recv_proj)
        return carry

    lax.fori_loop(0, ED // EF, recv_term, 0)
    prow = dot_nt(pickb, quad)
    pq = iota((ND, 4 * LN), 1) % 4
    pn = iota((ND, 4 * LN), 0).astype(F32)
    frow4 = jnp.broadcast_to(from_ref[...], (4 * LN, ND))
    fq = iota((4 * LN, ND), 0)
    for c in range(4):
        back_o[c * ND : (c + 1) * ND, :] = onehot((prow == pn) & (pq == c))
        back_p[:, c * ND : (c + 1) * ND] = onehot((frow4 - ND) * 4 + c == fq)
    for c in loads[2:]:
        c.wait()

    for c in gathers:
        c.wait_recv()
    for c in halos:
        c.wait_recv()

    def edge_forward(b, carry):
        rows = pl.ds(pl.multiple_of(b * EF, EF), EF)
        send_rows = dot(sel_s[rows, :], table[...]).astype(BF16)
        a, da = silu_pair(pre[rows, :] + dot(send_rows, ein[H : 2 * H, :]))
        a = a.astype(BF16)
        act[rows, :] = a
        dsilu[rows, :] = da
        yn, inv = norm(dot(a, eout[...]))
        normed[rows, :] = yn
        einv[rows, :] = jnp.broadcast_to(inv, (EF, LN))
        enew[rows, :] = (e[rows, :].astype(F32) + yn).astype(BF16)
        return carry

    lax.fori_loop(0, ED // EF, edge_forward, 0)

    agg = dot(sel_rt[...], enew[...]).astype(BF16)
    node_act, node_dsilu = silu_pair(dot(latent, nin[:H, :]) + dot(agg, nin[H:, :]))
    node_act = node_act.astype(BF16)
    nnorm, ninv = norm(dot(node_act, nout[...]))
    nodeup_ref[...] = (latent.astype(F32) + nnorm).astype(BF16)
    ncot = ncot_ref[...].astype(F32)
    nlg = norm_grad(nnorm, ninv, ncot).astype(BF16)
    npg = (dot_nt(nlg, nout[...]) * node_dsilu).astype(BF16)
    agh, agl = hi_lo(dot_nt(npg, nin[H:, :]))
    agg_grad = jnp.concatenate([agh, agl], 0)
    node_direct = ncot + dot_nt(npg, nin[:H, :])
    wg[4 * H : 5 * H, :] = dot_tn(latent, npg)
    wg[5 * H : 6 * H, :] = dot_tn(agg, npg)
    wg[6 * H :, :] = dot_tn(node_act, nlg)

    def two_blocks(block, k, side):
        base = 2 * SUB * block + 4 * 56 * k + 56 * side
        return jnp.concatenate(
            [
                wg[pl.ds(pl.multiple_of(base, 8), 56), :],
                wg[pl.ds(pl.multiple_of(base + 112, 8), 56), :],
            ],
            0,
        )

    def core_copy(block):
        rows = pl.ds(SUB * block, SUB)
        return remote(
            csend.at[rows], crecv.at[rows], c_s.at[block], c_r.at[block], sib, x
        )

    def pack_core(block):
        for k in range(2):
            rows = pl.ds(SUB * block + 112 * k, 112)
            csend[rows, :] = two_blocks(block, k, 1 - core).astype(BF16)
        core_copy(block).start()

    def columns(t):
        return pl.ds(pl.multiple_of(t * LN, LN), LN)

    def x1_copy(block, j):
        t = xpeer(j)
        i = 3 * block + j - 1
        return remote(
            chip.at[pl.ds(SUB * block, RX), columns(t)], rx.at[i], x1_s.at[i], x1_r.at[i], p, t
        )

    def y_copy(src, dst, ss, rs, block):
        i = 2 * (lax.rem(block // 2 - y + NY, NY) - 1) + block % 2
        return remote(
            src, dst.at[i], ss.at[i], rs.at[i], p + (block // 2 - y) * NC * NZ, x
        )

    def y1_copy(block):
        return y_copy(chip.at[pl.ds(SUB * block + RX, RY)], ry1, y1_s, y1_r, block)

    def y2_copy(block):
        return y_copy(bx.at[block], ry, y2_s, y2_r, block)

    def x2_copy(s, j):
        t = xpeer(j)
        i = 3 * s + j - 1
        return remote(b1.at[s, :, columns(t)], rx2.at[i], x2_s.at[i], x2_r.at[i], p, t)

    def y_block(j, s):
        return 2 * lax.rem(y + j, NY) + s

    def combine(block):
        core_copy(block).wait_recv()
        for k in range(2):
            rows = pl.ds(SUB * block + 112 * k, 112)
            chip[rows, :] = (
                two_blocks(block, k, core) + crecv[rows, :].astype(F32)
            ).astype(BF16)

        @pl.when(y != block // 2)
        def _():
            y1_copy(block).start()

        for j in (1, 3, 2):
            x1_copy(block, j).start()

    mine = columns(x)

    def finish_x(block):
        total = chip[pl.ds(SUB * block, RX), mine].astype(F32)
        for j in (1, 3, 2):
            x1_copy(block, j).wait_recv()
            total += rx[3 * block + j - 1].astype(F32)
        bx[block] = total.astype(BF16)

        @pl.when(y != block // 2)
        def _():
            y2_copy(block).start()

    def finish_y(s):
        own = pl.ds(pl.multiple_of(SUB * (2 * y + s) + RX, 16), RY)
        total = chip[own, :].astype(F32)
        for j in range(1, NY):
            y1_copy(y_block(j, s)).wait_recv()
            total += ry1[2 * (j - 1) + s].astype(F32)
        b1[s] = total.astype(BF16)
        for j in (1, 3, 2):
            x2_copy(s, j).start()

    for block in (7, 6, 5):
        pack_core(block)

    def edge_backward(b, carry):
        rows = pl.ds(pl.multiple_of(b * EB, EB), EB)
        upst = cot[rows, :].astype(F32) + dot(sel_r[rows, :], agg_grad)
        g = norm_grad(normed[rows, :], einv[rows, :1], upst).astype(BF16)
        plg[rows, :] = g
        pg = (dot_nt(g, eout[...]) * dsilu[rows, :]).astype(BF16)
        ppg[rows, :] = pg
        egrad[rows, :] = (upst + dot_nt(pg, ein[:H, :])).astype(BF16)
        return carry

    lax.fori_loop(0, 1, edge_backward, 0)
    for block in (7, 6, 5):
        combine(block)
    lax.fori_loop(1, ED // EB, edge_backward, 0)
    gsum[...] = dot(sel_st[...], ppg[...])
    gs[...] = gsum[...].astype(BF16)

    def own_of(t):
        return pl.ds(pl.multiple_of(t * ND, ND), ND)

    scatters = [
        remote(gs.at[own_of(xpeer(j))], gr.at[j - 1], g_s.at[j], g_r.at[j], p, xpeer(j))
        for j in (1, 3, 2)
    ] + [
        remote(gs.at[pl.ds(512, 16)], hb.at[pl.ds(16, 16)], g_s.at[0], g_r.at[0], dn, x),
        remote(gs.at[pl.ds(528, 16)], hb.at[pl.ds(0, 16)], g_s.at[4], g_r.at[4], up, x),
    ]
    for c in scatters:
        c.start()
    wg[3 * H : 4 * H, :] = dot_tn(act[...], plg[...])
    grecv = dot(sel_rt[...], ppg[...]).astype(BF16)
    wg[2 * H : 3 * H, :] = dot_tn(latent, grecv)
    pack_core(3)
    wg[H : 2 * H, :] = dot_tn(table[...], gs[...])
    wg[:H, :] = dot_tn(e[...], ppg[...])
    for block in (1, 2, 0, 4):
        pack_core(block)
    node_part = node_direct + dot_nt(grecv, ein[2 * H :, :])
    for block in (3, 1, 2, 0, 4):
        combine(block)
    for block in (7, 6, 5):
        finish_x(block)

    for c in scatters:
        c.wait_recv()
    crow = jnp.broadcast_to(cut_ref[...], (ND, 32))
    total = dot(onehot(crow == iota((ND, 32), 0)), hb[...])
    total += gsum[own_rows, :]
    for j in range(3):
        total += gr[j].astype(F32)
    node_grad = (node_part + dot_nt(total.astype(BF16), ein[H : 2 * H, :])).astype(BF16)
    ng = jnp.concatenate([node_grad[:, c * LN : (c + 1) * LN] for c in range(4)], 0)
    msgb[...] = dot(back_p[...], ng).reshape(DOM, 8, LN).astype(BF16)

    exchange(msgb, incb, rb_s, rb_r)

    def z_copy(t):
        i = lax.rem(t - z + NZ, NZ) - 1
        return remote(zp.at[t], rz.at[i], z_s.at[i], z_r.at[i], p + (t - z) * NC, x)

    def half_sum(s):
        part = bx[2 * y + s].astype(F32)
        for j in range(1, NY):
            y2_copy(y_block(j, s)).wait_recv()
            part += ry[2 * (j - 1) + s].astype(F32)
        rest = b1[s, :, mine].astype(F32)
        for j in (1, 3, 2):
            x2_copy(s, j).wait_recv()
            rest += rx2[3 * s + j - 1].astype(F32)
        total = jnp.concatenate([part, rest], 0)
        zown[SUB * s : SUB * (s + 1), :] = total
        for k in range(4):
            zp[4 * s + k] = jnp.concatenate(
                [total[56 * k : 56 * k + 56, :], jnp.zeros((8, LN), F32)], 0
            ).astype(BF16)
        for k in range(4):
            t = 4 * s + k

            @pl.when(t != z)
            def _():
                z_copy(t).start()

    for block in (3, 1):
        finish_x(block)
    finish_y(1)
    for block in (4, 2, 0):
        finish_x(block)
    finish_y(0)
    half_sum(1)
    half_sum(0)

    pltpu.make_async_copy(incb.at[pl.ds(0, DOM - 1)], incb.at[pl.ds(0, DOM - 1)], rb_r).wait()
    back = incb[...].astype(F32).reshape(4 * LN, LN).astype(BF16)
    slots = dot(back_o[...], back)
    stay_t = onehot(frow == iota((LN, ND), 0))
    latgrad_ref[...] = jnp.concatenate(
        [
            (
                dot(stay_t, node_grad[:, c * LN : (c + 1) * LN])
                + slots[c * ND : (c + 1) * ND, :]
            ).astype(BF16)
            for c in range(4)
        ],
        1,
    )

    total = zown[pl.ds(pl.multiple_of(56 * z, 8), 56), :]
    for j in range(1, NZ):
        z_copy(lax.rem(z + j, NZ)).wait_recv()
        total += rz[j - 1].astype(F32)[:56, :]
    wgrad_ref[...] = total

    pltpu.make_async_copy(msg.at[pl.ds(0, DOM - 1)], msg.at[pl.ds(0, DOM - 1)], r_s).wait()
    pltpu.make_async_copy(msgb.at[pl.ds(0, DOM - 1)], msgb.at[pl.ds(0, DOM - 1)], rb_s).wait()
    for c in gathers + halos + scatters:
        c.wait_send()
    for block in range(8):
        core_copy(block).wait_send()
        for j in (1, 3, 2):
            x1_copy(block, j).wait_send()
    for s in range(2):
        for j in range(1, NY):
            y1_copy(y_block(j, s)).wait_send()
            y2_copy(y_block(j, s)).wait_send()
            x2_copy(s, j).wait_send()
    for j in range(1, NZ):
        z_copy(lax.rem(z + j, NZ)).wait_send()


def hand_over(*refs):
    sem = refs[-1]
    copies = [
        pltpu.make_async_copy(a, b, sem.at[i])
        for i, (a, b) in enumerate(zip(refs[:5], refs[5:10]))
    ]
    for c in copies:
        c.start()
    for c in copies:
        c.wait()


def body(
    tile_latent, relay_pick, relay_from, cut_pick, edge_latent, edge_sender, edge_receiver,
    edge_in, edge_out, node_in, node_out, node_cot, edge_cot,
):
    vmem = pl.BlockSpec(memory_space=pltpu.VMEM)
    hbm = pl.BlockSpec(memory_space=pl.ANY)
    dma = pltpu.SemaphoreType.DMA
    V = pltpu.VMEM
    scratch = [
        V((ED, H), BF16), V((ED, H), BF16), V((3 * H, H), BF16), V((H, H), BF16),
        V((2 * H, H), BF16), V((H, H), BF16), dma((8,)),
        V((DOM, 8, LN), BF16), V((DOM, 8, LN), BF16), V((DOM, 8, LN), BF16), V((DOM, 8, LN), BF16),
        V((TR, H), BF16), V((ND, H), BF16), V((32, H), BF16),
        V((ED, TR), BF16), V((TR, ED), BF16), V((ED, 2 * LN), BF16), V((ND, ED), BF16),
        V((4 * ND, 4 * LN), BF16), V((4 * ND, 4 * LN), BF16), V((4 * LN, 4 * ND), BF16),
        V((ED, H), F32), V((ED, H), BF16), V((ED, H), F32), V((ED, H), F32), V((ED, LN), F32),
        V((ED, H), BF16), V((ED, H), BF16),
        V((TR, H), F32), V((TR, H), BF16), V((3, ND, H), BF16), V((32, H), BF16), V((7 * H, H), F32),
        V((8 * SUB, H), BF16), V((8 * SUB, H), BF16), V((8 * SUB, H), BF16),
        V((24, RX, LN), BF16), V((8, RX, LN), BF16), V((6, RX, LN), BF16),
        V((6, RY, H), BF16), V((2, RY, H), BF16), V((6, RY, LN), BF16),
        V((2 * SUB, LN), F32), V((NZ, 64, LN), BF16), V((NZ - 1, 64, LN), BF16),
        dma, dma, dma((5,)), dma((5,)), dma, dma, dma((5,)), dma((5,)), dma((8,)), dma((8,)),
        dma((24,)), dma((24,)), dma((6,)), dma((6,)), dma((6,)), dma((6,)), dma((6,)), dma((6,)),
        dma((NZ - 1,)), dma((NZ - 1,)),
    ]
    held = tuple(
        pltpu.VMEM(s, d)
        for s, d in (
            ((ND, H), BF16), ((ED, H), BF16), ((ND, H), BF16), ((ED, H), BF16), ((56, LN), F32),
        )
    )
    shapes = (
        jax.ShapeDtypeStruct((ND, H), BF16),
        jax.ShapeDtypeStruct((ED, H), BF16),
        jax.ShapeDtypeStruct((ND, H), BF16),
        jax.ShapeDtypeStruct((ED, H), BF16),
        jax.ShapeDtypeStruct((56, LN), F32),
    )
    parts = pl.pallas_call(
        kernel,
        out_shape=held,
        in_specs=[vmem] * 7 + [hbm] * 6,
        out_specs=(vmem,) * 5,
        scratch_shapes=scratch,
        compiler_params=pltpu.CompilerParams(
            collective_id=0, has_side_effects=True, vmem_limit_bytes=56 * 2**20
        ),
    )(
        tile_latent, relay_pick, relay_from.reshape(1, ND), cut_pick,
        edge_sender.reshape(ED // LN, LN), edge_receiver.reshape(ED // LN, LN), node_cot,
        edge_latent, edge_cot, edge_in, edge_out, node_in, node_out,
    )
    return pl.pallas_call(
        hand_over,
        out_shape=shapes,
        in_specs=[vmem] * 5,
        out_specs=(hbm,) * 5,
        scratch_shapes=[dma((5,))],
        compiler_params=pltpu.CompilerParams(vmem_limit_bytes=2**20),
    )(*parts)


def solution(mesh):
    rows = P(("dom", "tile"), None)
    flat = P(("dom", "tile"))
    in_specs = (
        rows, rows, flat, rows, rows, flat, flat, P(), P(), P(), P(), rows, rows,
    )
    out_specs = (rows, rows, rows, rows, P("dom", "tile"))
    return jax.shard_map(body, mesh=mesh, in_specs=in_specs, out_specs=out_specs, check_vma=False)
```

```python
import jax
import jax.numpy as jnp
from jax import lax
from jax.experimental import pallas as pl
from jax.experimental.pallas import tpu as pltpu
from jax.sharding import PartitionSpec as P

EPSILON = 1e-05
MESH = pl.DeviceIdType.MESH
F32 = jnp.float32
BF16 = jnp.bfloat16
NX, NY, NZ, NC = 4, 4, 8, 2
DOM = NY * NZ * NC
H = 512
ND = 128
ED = 768
EB = 384
EF = 768
TR = 640
LN = 128
SUB = 224
RX = 112
RY = SUB - RX


def iota(shape, dim):
    return lax.broadcasted_iota(jnp.int32, shape, dim)


def onehot(mask):
    return jnp.where(mask, 1.0, 0.0).astype(BF16)


def dot(a, b):
    return lax.dot_general(a, b, (((1,), (0,)), ((), ())), preferred_element_type=F32)


def dot_nt(a, b):
    return lax.dot_general(a, b, (((1,), (1,)), ((), ())), preferred_element_type=F32)


def dot_tn(a, b):
    return lax.dot_general(a, b, (((0,), (0,)), ((), ())), preferred_element_type=F32)


def norm(v):
    center = v - jnp.mean(v, -1, keepdims=True)
    inv = lax.rsqrt(jnp.mean(center * center, -1, keepdims=True) + EPSILON)
    return center * inv, inv


def norm_grad(normed, inv, up):
    mean_up = jnp.mean(up, -1, keepdims=True)
    mean_cross = jnp.mean(up * normed, -1, keepdims=True)
    return inv * (up - mean_up - normed * mean_cross)


def silu_pair(v):
    sig = 1.0 / (1.0 + jnp.exp(-v))
    act = v * sig
    return act, sig + act * (1.0 - sig)


def hi_lo(v):
    hi = v.astype(BF16)
    return hi, (v - hi.astype(F32)).astype(BF16)


def kernel(
    tile_hbm, pick_hbm, from_hbm, cut_ref, snd_hbm, rcv_hbm, ncot_hbm,
    e_hbm, cot_hbm, ein_hbm, eout_hbm, nin_hbm, nout_hbm,
    nodeup_ref, enew, latgrad_ref, egrad, wgrad_ref,
    e, cot, ein, eout, nin, nout, tile_ref, pick_ref, from_ref, snd_ref, rcv_ref, ncot_ref, lsem,
    nbase,
    msg, inc, msgb, incb, table, lat, halo_s,
    sel_s, sel_st, sel_r, sel_rt, gat_i, back_o, back_p,
    pre, act, dsilu, normed, einv, plg, ppg,
    gsum, gs, gr, hb, wg,
    csend, crecv, chip, rx, bx, ry, ry1, b1, rx2, zown, zp, rz,
    r_s, r_r, a_s, a_r, rb_s, rb_r, g_s, g_r, c_s, c_r,
    x1_s, x1_r, y1_s, y1_r, y2_s, y2_r, x2_s, x2_r, z_s, z_r,
):
    p = lax.axis_index("dom")
    x = lax.axis_index("tile")
    core = lax.rem(p, NC)
    z = lax.rem(p // NC, NZ)
    y = p // (NC * NZ)
    up = lax.rem(p + 1, DOM)
    dn = lax.rem(p + DOM - 1, DOM)
    sib = p + 1 - 2 * core

    def xpeer(j):
        return lax.rem(x + j, NX)

    def remote(src, dst, ss, rs, d, t):
        return pltpu.make_async_remote_copy(
            src, dst, ss, rs, device_id=(d, t), device_id_type=MESH
        )

    first = [
        pltpu.make_async_copy(s, d, lsem.at[6 + i])
        for i, (s, d) in enumerate(
            (
                (tile_hbm, tile_ref), (pick_hbm, pick_ref), (from_hbm, from_ref),
                (snd_hbm, snd_ref), (rcv_hbm, rcv_ref), (ncot_hbm, ncot_ref),
            )
        )
    ]
    for c in first:
        c.start()

    barrier = pltpu.get_barrier_semaphore()

    def greet(i, carry):
        pl.semaphore_signal(
            barrier, 1, device_id=(lax.rem(p + i, DOM), x), device_id_type=MESH
        )
        return carry

    lax.fori_loop(1, DOM, greet, 0)
    for j in range(1, NX):
        pl.semaphore_signal(barrier, 1, device_id=(p, xpeer(j)), device_id_type=MESH)

    loads = [
        pltpu.make_async_copy(s, d, lsem.at[i])
        for i, (s, d) in enumerate(
            (
                (e_hbm, e), (ein_hbm, ein), (eout_hbm, eout), (nin_hbm, nin),
                (nout_hbm, nout), (cot_hbm, cot),
            )
        )
    ]
    for c in loads:
        c.start()

    first[0].wait()
    first[1].wait()
    pickb = jnp.broadcast_to(pick_ref[...], (ND, LN)).astype(F32).astype(BF16)
    quad = onehot(iota((4 * LN, LN), 0) // 4 == iota((4 * LN, LN), 1))
    rep = dot_nt(quad, pickb)
    qlane = iota((4 * LN, LN), 1).astype(F32)
    qmod = iota((4 * LN, LN), 0) % 4
    out = jnp.zeros((4 * LN, LN), F32)
    for c in range(4):
        out += dot(
            onehot((rep == qlane) & (qmod == c)), tile_ref[:, c * LN : (c + 1) * LN]
        )
    msg[...] = out.reshape(DOM, 8, LN).astype(BF16)
    inc[p] = jnp.zeros((8, LN), BF16)
    incb[p] = jnp.zeros((8, LN), BF16)

    pl.semaphore_wait(barrier, DOM - 1 + NX - 1)

    def exchange(src, dst, ss, rs):
        def step(i, last):
            dz = NZ // 2 + (i + 1) // 2 * (1 - 2 * (i % 2))
            for dy in (2, 1, 3, 0):
                for dc in (0, 1):
                    if not last or dy or dc:
                        q = lax.rem(y + dy, NY) * (NZ * NC)
                        q += lax.rem(z + dz, NZ) * NC + lax.rem(core + dc, NC)
                        remote(src.at[q], dst.at[p], ss, rs, q, x).start()

        def loop(i, carry):
            step(i, False)
            return carry

        lax.fori_loop(0, NZ - 1, loop, 0)
        step(NZ - 1, True)

    exchange(msg, inc, r_s, r_r)

    for c in first[2:]:
        c.wait()
    frow = jnp.broadcast_to(from_ref[...], (LN, ND))
    fcol = frow.T
    fcol4 = jnp.concatenate([fcol] * 4, 1)
    for c in range(4):
        gat_i[c * ND : (c + 1) * ND, :] = onehot(
            (fcol4 - ND) * 4 + c == iota((ND, 4 * LN), 1)
        )
    stay = onehot(fcol == iota((ND, LN), 1))

    lane = iota((LN, LN), 1)
    subl = iota((LN, LN), 0)

    def selections(b, carry):
        rows = pl.ds(pl.multiple_of(b * LN, LN), LN)
        srow = jnp.broadcast_to(snd_ref[pl.ds(b, 1), :], (LN, LN))
        rrow = jnp.broadcast_to(rcv_ref[pl.ds(b, 1), :], (LN, LN))
        scol = srow.T
        rcol = rrow.T
        for k in range(TR // LN):
            sel_s[rows, k * LN : (k + 1) * LN] = onehot(scol == lane + k * LN)
            sel_st[k * LN : (k + 1) * LN, rows] = onehot(srow == subl + k * LN)
        r = onehot(rcol == lane)
        sel_r[rows, :LN] = r
        sel_r[rows, LN:] = r
        sel_rt[:, rows] = onehot(rrow == subl)
        return carry

    lax.fori_loop(0, ED // LN, selections, 0)
    table[pl.ds(NX * ND + 32, TR - NX * ND - 32), :] = jnp.zeros((TR - NX * ND - 32, H), BF16)

    loads[0].wait()
    loads[1].wait()

    def edge_term(b, carry):
        rows = pl.ds(pl.multiple_of(b * EF, EF), EF)
        pre[rows, :] = dot(e[rows, :], ein[:H, :])
        return carry

    lax.fori_loop(0, ED // EF, edge_term, 0)

    pltpu.make_async_copy(inc.at[pl.ds(0, DOM - 1)], inc.at[pl.ds(0, DOM - 1)], r_r).wait()
    got = inc[...].astype(F32).reshape(4 * LN, LN).astype(BF16)
    slots = dot(gat_i[...], got)
    latent = jnp.concatenate(
        [
            (
                dot(stay, tile_ref[:, c * LN : (c + 1) * LN])
                + slots[c * ND : (c + 1) * ND, :]
            ).astype(BF16)
            for c in range(4)
        ],
        1,
    )
    lat[...] = latent
    own_rows = pl.ds(pl.multiple_of(x * ND, ND), ND)
    table[own_rows, :] = latent

    half_rows = ND // 2

    def piece(t, part):
        return table.at[pl.ds(pl.multiple_of(t * ND + part * half_rows, half_rows), half_rows)]

    def gather_copy(t, part, j, i):
        return remote(piece(t, part), piece(t, part), a_s.at[i], a_r.at[i], p, xpeer(j))

    def arrived(t, part, i):
        pltpu.make_async_copy(piece(t, part), piece(t, part), a_r.at[i]).wait()

    gathers = [
        gather_copy(x, 0, 1, 0), gather_copy(x, 1, 3, 2),
        gather_copy(x, 1, 1, 1), gather_copy(x, 0, 3, 3),
    ]
    for c in gathers:
        c.start()
    cutb = jnp.broadcast_to(cut_ref[...], (LN, 32)).astype(F32).astype(BF16)
    eye = onehot(iota((32, 32), 0) == iota((32, 32), 1))
    ccol = dot_nt(eye, cutb)
    halo_s[...] = dot(onehot(ccol == iota((32, LN), 1).astype(F32)), latent).astype(BF16)
    halos = [
        remote(halo_s.at[pl.ds(16, 16)], table.at[pl.ds(512, 16)], a_s.at[6], a_r.at[6], up, x),
        remote(halo_s.at[pl.ds(0, 16)], table.at[pl.ds(528, 16)], a_s.at[7], a_r.at[7], dn, x),
    ]
    for c in halos:
        c.start()

    rh, rl = hi_lo(dot(latent, ein[2 * H :, :]))
    recv_proj = jnp.concatenate([rh, rl], 0)

    def recv_term(b, carry):
        rows = pl.ds(pl.multiple_of(b * EF, EF), EF)
        pre[rows, :] += dot(sel_r[rows, :], recv_proj)
        return carry

    lax.fori_loop(0, ED // EF, recv_term, 0)
    prow = dot_nt(pickb, quad)
    pq = iota((ND, 4 * LN), 1) % 4
    pn = iota((ND, 4 * LN), 0).astype(F32)
    frow4 = jnp.broadcast_to(from_ref[...], (4 * LN, ND))
    fq = iota((4 * LN, ND), 0)
    for c in range(4):
        back_o[c * ND : (c + 1) * ND, :] = onehot((prow == pn) & (pq == c))
        back_p[:, c * ND : (c + 1) * ND] = onehot((frow4 - ND) * 4 + c == fq)
    for c in loads[2:]:
        c.wait()
    nbase[...] = dot(latent, nin[:H, :])

    arrived(xpeer(3), 0, 0)
    forwards = [gather_copy(xpeer(3), 0, 1, 4)]
    forwards[0].start()
    arrived(xpeer(1), 1, 2)
    forwards.append(gather_copy(xpeer(1), 1, 3, 5))
    forwards[1].start()
    arrived(xpeer(3), 1, 1)
    arrived(xpeer(1), 0, 3)
    arrived(xpeer(2), 0, 4)
    arrived(xpeer(2), 1, 5)
    for c in halos:
        c.wait_recv()

    def edge_forward(b, carry):
        rows = pl.ds(pl.multiple_of(b * EF, EF), EF)
        send_rows = dot(sel_s[rows, :], table[...]).astype(BF16)
        a, da = silu_pair(pre[rows, :] + dot(send_rows, ein[H : 2 * H, :]))
        a = a.astype(BF16)
        act[rows, :] = a
        dsilu[rows, :] = da
        yn, inv = norm(dot(a, eout[...]))
        normed[rows, :] = yn
        einv[rows, :] = jnp.broadcast_to(inv, (EF, LN))
        enew[rows, :] = (e[rows, :].astype(F32) + yn).astype(BF16)
        return carry

    lax.fori_loop(0, ED // EF, edge_forward, 0)

    agg = dot(sel_rt[...], enew[...]).astype(BF16)
    node_act, node_dsilu = silu_pair(nbase[...] + dot(agg, nin[H:, :]))
    node_act = node_act.astype(BF16)
    nnorm, ninv = norm(dot(node_act, nout[...]))
    nodeup_ref[...] = (latent.astype(F32) + nnorm).astype(BF16)
    ncot = ncot_ref[...].astype(F32)
    nlg = norm_grad(nnorm, ninv, ncot).astype(BF16)
    npg = (dot_nt(nlg, nout[...]) * node_dsilu).astype(BF16)
    agh, agl = hi_lo(dot_nt(npg, nin[H:, :]))
    agg_grad = jnp.concatenate([agh, agl], 0)
    wg[4 * H : 5 * H, :] = dot_tn(latent, npg)
    wg[5 * H : 6 * H, :] = dot_tn(agg, npg)
    wg[6 * H :, :] = dot_tn(node_act, nlg)

    def two_blocks(block, k, side):
        base = 2 * SUB * block + 4 * 56 * k + 56 * side
        return jnp.concatenate(
            [
                wg[pl.ds(pl.multiple_of(base, 8), 56), :],
                wg[pl.ds(pl.multiple_of(base + 112, 8), 56), :],
            ],
            0,
        )

    def core_copy(block):
        rows = pl.ds(SUB * block, SUB)
        return remote(
            csend.at[rows], crecv.at[rows], c_s.at[block], c_r.at[block], sib, x
        )

    def pack_core(block):
        for k in range(2):
            rows = pl.ds(SUB * block + 112 * k, 112)
            csend[rows, :] = two_blocks(block, k, 1 - core).astype(BF16)
        core_copy(block).start()

    def columns(t):
        return pl.ds(pl.multiple_of(t * LN, LN), LN)

    def x1_copy(block, j):
        t = xpeer(j)
        i = 3 * block + j - 1
        return remote(
            chip.at[pl.ds(SUB * block, RX), columns(t)], rx.at[i], x1_s.at[i], x1_r.at[i], p, t
        )

    def y_copy(src, dst, ss, rs, block):
        i = 2 * (lax.rem(block // 2 - y + NY, NY) - 1) + block % 2
        return remote(
            src, dst.at[i], ss.at[i], rs.at[i], p + (block // 2 - y) * NC * NZ, x
        )

    def y1_copy(block):
        return y_copy(chip.at[pl.ds(SUB * block + RX, RY)], ry1, y1_s, y1_r, block)

    def y2_copy(block):
        return y_copy(bx.at[block], ry, y2_s, y2_r, block)

    def x2_copy(s, j):
        t = xpeer(j)
        i = 3 * s + j - 1
        return remote(b1.at[s, :, columns(t)], rx2.at[i], x2_s.at[i], x2_r.at[i], p, t)

    def y_block(j, s):
        return 2 * lax.rem(y + j, NY) + s

    def combine(block):
        core_copy(block).wait_recv()
        for k in range(2):
            rows = pl.ds(SUB * block + 112 * k, 112)
            chip[rows, :] = (
                two_blocks(block, k, core) + crecv[rows, :].astype(F32)
            ).astype(BF16)

        @pl.when(y != block // 2)
        def _():
            y1_copy(block).start()

        for j in (1, 3, 2):
            x1_copy(block, j).start()

    mine = columns(x)

    def finish_x(block):
        total = chip[pl.ds(SUB * block, RX), mine].astype(F32)
        for j in (1, 3, 2):
            x1_copy(block, j).wait_recv()
            total += rx[3 * block + j - 1].astype(F32)
        bx[block] = total.astype(BF16)

        @pl.when(y != block // 2)
        def _():
            y2_copy(block).start()

    def finish_y(s):
        own = pl.ds(pl.multiple_of(SUB * (2 * y + s) + RX, 16), RY)
        total = chip[own, :].astype(F32)
        for j in range(1, NY):
            y1_copy(y_block(j, s)).wait_recv()
            total += ry1[2 * (j - 1) + s].astype(F32)
        b1[s] = total.astype(BF16)
        for j in (1, 3, 2):
            x2_copy(s, j).start()

    for block in (7, 6, 5):
        pack_core(block)

    def edge_backward(b, carry):
        rows = pl.ds(pl.multiple_of(b * EB, EB), EB)
        upst = cot[rows, :].astype(F32) + dot(sel_r[rows, :], agg_grad)
        g = norm_grad(normed[rows, :], einv[rows, :1], upst).astype(BF16)
        plg[rows, :] = g
        pg = (dot_nt(g, eout[...]) * dsilu[rows, :]).astype(BF16)
        ppg[rows, :] = pg
        return carry

    lax.fori_loop(0, 1, edge_backward, 0)
    for block in (7, 6, 5):
        combine(block)
    lax.fori_loop(1, ED // EB, edge_backward, 0)
    def own_of(t):
        return pl.ds(pl.multiple_of(t * ND, ND), ND)

    scatters = [
        remote(gs.at[own_of(xpeer(j))], gr.at[j - 1], g_s.at[j], g_r.at[j], p, xpeer(j))
        for j in (1, 3, 2)
    ] + [
        remote(gs.at[pl.ds(512, 16)], hb.at[pl.ds(16, 16)], g_s.at[0], g_r.at[0], dn, x),
        remote(gs.at[pl.ds(528, 16)], hb.at[pl.ds(0, 16)], g_s.at[4], g_r.at[4], up, x),
    ]
    wg[:H, :] = dot_tn(e[...], ppg[...])
    pack_core(0)
    grecv = dot(sel_rt[...], ppg[...]).astype(BF16)
    wg[2 * H : 3 * H, :] = dot_tn(latent, grecv)
    gsum[...] = dot(sel_st[...], ppg[...])
    gs[...] = gsum[...].astype(BF16)
    wg[H : 2 * H, :] = dot_tn(table[...], gs[...])
    pack_core(2)
    pack_core(1)
    wg[3 * H : 4 * H, :] = dot_tn(act[...], plg[...])
    pack_core(3)
    pack_core(4)
    for c in scatters:
        c.start()
    for block in (0, 2, 1, 3, 4):
        combine(block)

    def edge_result(b, carry):
        rows = pl.ds(pl.multiple_of(b * EB, EB), EB)
        total = cot[rows, :].astype(F32) + dot(sel_r[rows, :], agg_grad)
        egrad[rows, :] = (total + dot_nt(ppg[rows, :], ein[:H, :])).astype(BF16)
        return carry

    lax.fori_loop(0, ED // EB, edge_result, 0)
    node_direct = ncot + dot_nt(npg, nin[:H, :])
    node_part = node_direct + dot_nt(grecv, ein[2 * H :, :])

    for c in scatters:
        c.wait_recv()
    crow = jnp.broadcast_to(cut_ref[...], (ND, 32))
    total = dot(onehot(crow == iota((ND, 32), 0)), hb[...])
    total += gsum[own_rows, :]
    for j in range(3):
        total += gr[j].astype(F32)
    node_grad = (node_part + dot_nt(total.astype(BF16), ein[H : 2 * H, :])).astype(BF16)
    ng = jnp.concatenate([node_grad[:, c * LN : (c + 1) * LN] for c in range(4)], 0)
    msgb[...] = dot(back_p[...], ng).reshape(DOM, 8, LN).astype(BF16)

    exchange(msgb, incb, rb_s, rb_r)
    for block in (7, 6, 5):
        finish_x(block)

    def z_copy(t):
        i = lax.rem(t - z + NZ, NZ) - 1
        return remote(zp.at[t], rz.at[i], z_s.at[i], z_r.at[i], p + (t - z) * NC, x)

    def half_sum(s):
        part = bx[2 * y + s].astype(F32)
        for j in range(1, NY):
            y2_copy(y_block(j, s)).wait_recv()
            part += ry[2 * (j - 1) + s].astype(F32)
        rest = b1[s, :, mine].astype(F32)
        for j in (1, 3, 2):
            x2_copy(s, j).wait_recv()
            rest += rx2[3 * s + j - 1].astype(F32)
        total = jnp.concatenate([part, rest], 0)
        zown[SUB * s : SUB * (s + 1), :] = total
        for k in range(4):
            zp[4 * s + k] = jnp.concatenate(
                [total[56 * k : 56 * k + 56, :], jnp.zeros((8, LN), F32)], 0
            ).astype(BF16)
        for k in range(4):
            t = 4 * s + k

            @pl.when(t != z)
            def _():
                z_copy(t).start()

    for block in (0, 2):
        finish_x(block)
    finish_y(0)
    for block in (1, 3, 4):
        finish_x(block)
    finish_y(1)
    half_sum(0)
    half_sum(1)

    pltpu.make_async_copy(incb.at[pl.ds(0, DOM - 1)], incb.at[pl.ds(0, DOM - 1)], rb_r).wait()
    back = incb[...].astype(F32).reshape(4 * LN, LN).astype(BF16)
    slots = dot(back_o[...], back)
    stay_t = onehot(frow == iota((LN, ND), 0))
    latgrad_ref[...] = jnp.concatenate(
        [
            (
                dot(stay_t, node_grad[:, c * LN : (c + 1) * LN])
                + slots[c * ND : (c + 1) * ND, :]
            ).astype(BF16)
            for c in range(4)
        ],
        1,
    )

    total = zown[pl.ds(pl.multiple_of(56 * z, 8), 56), :]
    for j in range(1, NZ):
        z_copy(lax.rem(z + j, NZ)).wait_recv()
        total += rz[j - 1].astype(F32)[:56, :]
    wgrad_ref[...] = total

    pltpu.make_async_copy(msg.at[pl.ds(0, DOM - 1)], msg.at[pl.ds(0, DOM - 1)], r_s).wait()
    pltpu.make_async_copy(msgb.at[pl.ds(0, DOM - 1)], msgb.at[pl.ds(0, DOM - 1)], rb_s).wait()
    for c in gathers + forwards + halos + scatters:
        c.wait_send()
    for block in range(8):
        core_copy(block).wait_send()
        for j in (1, 3, 2):
            x1_copy(block, j).wait_send()
    for s in range(2):
        for j in range(1, NY):
            y1_copy(y_block(j, s)).wait_send()
            y2_copy(y_block(j, s)).wait_send()
            x2_copy(s, j).wait_send()
    for j in range(1, NZ):
        z_copy(lax.rem(z + j, NZ)).wait_send()


def hand_over(*refs):
    sem = refs[-1]
    copies = [
        pltpu.make_async_copy(a, b, sem.at[i])
        for i, (a, b) in enumerate(zip(refs[:5], refs[5:10]))
    ]
    for c in copies:
        c.start()
    for c in copies:
        c.wait()


def body(
    tile_latent, relay_pick, relay_from, cut_pick, edge_latent, edge_sender, edge_receiver,
    edge_in, edge_out, node_in, node_out, node_cot, edge_cot,
):
    vmem = pl.BlockSpec(memory_space=pltpu.VMEM)
    hbm = pl.BlockSpec(memory_space=pl.ANY)
    pin = pl.BlockSpec(memory_space=pltpu.HBM)
    dma = pltpu.SemaphoreType.DMA
    V = pltpu.VMEM
    scratch = [
        V((ED, H), BF16), V((ED, H), BF16), V((3 * H, H), BF16), V((H, H), BF16),
        V((2 * H, H), BF16), V((H, H), BF16), V((ND, H), BF16), V((1, LN), jnp.int32),
        V((1, ND), jnp.int32), V((ED // LN, LN), jnp.int32), V((ED // LN, LN), jnp.int32),
        V((ND, H), BF16), dma((12,)), V((ND, H), F32),
        V((DOM, 8, LN), BF16), V((DOM, 8, LN), BF16), V((DOM, 8, LN), BF16), V((DOM, 8, LN), BF16),
        V((TR, H), BF16), V((ND, H), BF16), V((32, H), BF16),
        V((ED, TR), BF16), V((TR, ED), BF16), V((ED, 2 * LN), BF16), V((ND, ED), BF16),
        V((4 * ND, 4 * LN), BF16), V((4 * ND, 4 * LN), BF16), V((4 * LN, 4 * ND), BF16),
        V((ED, H), F32), V((ED, H), BF16), V((ED, H), F32), V((ED, H), F32), V((ED, LN), F32),
        V((ED, H), BF16), V((ED, H), BF16),
        V((TR, H), F32), V((TR, H), BF16), V((3, ND, H), BF16), V((32, H), BF16), V((7 * H, H), F32),
        V((8 * SUB, H), BF16), V((8 * SUB, H), BF16), V((8 * SUB, H), BF16),
        V((24, RX, LN), BF16), V((8, RX, LN), BF16), V((6, RX, LN), BF16),
        V((6, RY, H), BF16), V((2, RY, H), BF16), V((6, RY, LN), BF16),
        V((2 * SUB, LN), F32), V((NZ, 64, LN), BF16), V((NZ - 1, 64, LN), BF16),
        dma, dma, dma((8,)), dma((8,)), dma, dma, dma((5,)), dma((5,)), dma((8,)), dma((8,)),
        dma((24,)), dma((24,)), dma((6,)), dma((6,)), dma((6,)), dma((6,)), dma((6,)), dma((6,)),
        dma((NZ - 1,)), dma((NZ - 1,)),
    ]
    held = tuple(
        pltpu.VMEM(s, d)
        for s, d in (
            ((ND, H), BF16), ((ED, H), BF16), ((ND, H), BF16), ((ED, H), BF16), ((56, LN), F32),
        )
    )
    shapes = (
        jax.ShapeDtypeStruct((ND, H), BF16),
        jax.ShapeDtypeStruct((ED, H), BF16),
        jax.ShapeDtypeStruct((ND, H), BF16),
        jax.ShapeDtypeStruct((ED, H), BF16),
        jax.ShapeDtypeStruct((56, LN), F32),
    )
    parts = pl.pallas_call(
        kernel,
        out_shape=held,
        in_specs=[pin] * 3 + [vmem] + [pin] * 3 + [hbm] * 6,
        out_specs=(vmem,) * 5,
        scratch_shapes=scratch,
        compiler_params=pltpu.CompilerParams(
            collective_id=0, has_side_effects=True, vmem_limit_bytes=56 * 2**20
        ),
    )(
        tile_latent, relay_pick, relay_from.reshape(1, ND), cut_pick,
        edge_sender.reshape(ED // LN, LN), edge_receiver.reshape(ED // LN, LN), node_cot,
        edge_latent, edge_cot, edge_in, edge_out, node_in, node_out,
    )
    return pl.pallas_call(
        hand_over,
        out_shape=shapes,
        in_specs=[vmem] * 5,
        out_specs=(hbm,) * 5,
        scratch_shapes=[dma((5,))],
        compiler_params=pltpu.CompilerParams(vmem_limit_bytes=2**20),
    )(*parts)


def solution(mesh):
    rows = P(("dom", "tile"), None)
    flat = P(("dom", "tile"))
    in_specs = (
        rows, rows, flat, rows, rows, flat, flat, P(), P(), P(), P(), rows, rows,
    )
    out_specs = (rows, rows, rows, rows, P("dom", "tile"))
    return jax.shard_map(body, mesh=mesh, in_specs=in_specs, out_specs=out_specs, check_vma=False)
```

```python
import jax
import jax.numpy as jnp
from jax import lax
from jax.experimental import pallas as pl
from jax.experimental.pallas import tpu as pltpu
from jax.sharding import PartitionSpec as P

EPSILON = 1e-05
MESH = pl.DeviceIdType.MESH
F32 = jnp.float32
BF16 = jnp.bfloat16
NX, NY, NZ, NC = 4, 4, 8, 2
DOM = NY * NZ * NC
H = 512
ND = 128
ED = 768
EB = 384
EF = 768
TR = 640
LN = 128
SUB = 224
RX = 112
RY = SUB - RX


def iota(shape, dim):
    return lax.broadcasted_iota(jnp.int32, shape, dim)


def onehot(mask):
    return jnp.where(mask, 1.0, 0.0).astype(BF16)


def dot(a, b):
    return lax.dot_general(a, b, (((1,), (0,)), ((), ())), preferred_element_type=F32)


def dot_nt(a, b):
    return lax.dot_general(a, b, (((1,), (1,)), ((), ())), preferred_element_type=F32)


def dot_tn(a, b):
    return lax.dot_general(a, b, (((0,), (0,)), ((), ())), preferred_element_type=F32)


def norm(v):
    center = v - jnp.mean(v, -1, keepdims=True)
    inv = lax.rsqrt(jnp.mean(center * center, -1, keepdims=True) + EPSILON)
    return center * inv, inv


def norm_grad(normed, inv, up):
    mean_up = jnp.mean(up, -1, keepdims=True)
    mean_cross = jnp.mean(up * normed, -1, keepdims=True)
    return inv * (up - mean_up - normed * mean_cross)


def silu_pair(v):
    sig = 1.0 / (1.0 + jnp.exp(-v))
    act = v * sig
    return act, sig + act * (1.0 - sig)


def hi_lo(v):
    hi = v.astype(BF16)
    return hi, (v - hi.astype(F32)).astype(BF16)


def kernel(
    tile_hbm, pick_hbm, from_hbm, cut_ref, snd_hbm, rcv_hbm, ncot_hbm,
    e_hbm, cot_hbm, ein_hbm, eout_hbm, nin_hbm, nout_hbm,
    nodeup_ref, enew, latgrad_ref, egrad, wgrad_ref,
    e, cot, ein, eout, nin, nout, tile_ref, pick_ref, from_ref, snd_ref, rcv_ref, ncot_ref, lsem,
    nbase,
    msg, inc, msgb, incb, table, lat, halo_s,
    sel_s, sel_st, sel_r, sel_rt, gat_i, back_o, back_p,
    pre, act, dsilu, normed, einv, plg, ppg,
    gsum, gs, gr, hb, wg,
    csend, crecv, chip, rx, bx, ry, ry1, b1, rx2, zown, zp, rz,
    r_s, r_r, a_s, a_r, rb_s, rb_r, g_s, g_r, c_s, c_r,
    x1_s, x1_r, y1_s, y1_r, y2_s, y2_r, x2_s, x2_r, z_s, z_r,
):
    p = lax.axis_index("dom")
    x = lax.axis_index("tile")
    core = lax.rem(p, NC)
    z = lax.rem(p // NC, NZ)
    y = p // (NC * NZ)
    up = lax.rem(p + 1, DOM)
    dn = lax.rem(p + DOM - 1, DOM)
    sib = p + 1 - 2 * core

    def xpeer(j):
        return lax.rem(x + j, NX)

    def remote(src, dst, ss, rs, d, t):
        return pltpu.make_async_remote_copy(
            src, dst, ss, rs, device_id=(d, t), device_id_type=MESH
        )

    first = [
        pltpu.make_async_copy(s, d, lsem.at[6 + i])
        for i, (s, d) in enumerate(
            (
                (tile_hbm, tile_ref), (pick_hbm, pick_ref), (from_hbm, from_ref),
                (snd_hbm, snd_ref), (rcv_hbm, rcv_ref), (ncot_hbm, ncot_ref),
            )
        )
    ]
    for c in first:
        c.start()

    barrier = pltpu.get_barrier_semaphore()

    def greet(i, carry):
        pl.semaphore_signal(
            barrier, 1, device_id=(lax.rem(p + i, DOM), x), device_id_type=MESH
        )
        return carry

    lax.fori_loop(1, DOM, greet, 0)
    for j in range(1, NX):
        pl.semaphore_signal(barrier, 1, device_id=(p, xpeer(j)), device_id_type=MESH)

    loads = [
        pltpu.make_async_copy(s, d, lsem.at[i])
        for i, (s, d) in enumerate(
            (
                (e_hbm, e), (ein_hbm, ein), (eout_hbm, eout), (nin_hbm, nin),
                (nout_hbm, nout), (cot_hbm, cot),
            )
        )
    ]
    for c in loads:
        c.start()

    first[0].wait()
    first[1].wait()
    pickb = jnp.broadcast_to(pick_ref[...], (ND, LN)).astype(F32).astype(BF16)
    quad = onehot(iota((4 * LN, LN), 0) // 4 == iota((4 * LN, LN), 1))
    rep = dot_nt(quad, pickb)
    qlane = iota((4 * LN, LN), 1).astype(F32)
    qmod = iota((4 * LN, LN), 0) % 4
    out = jnp.zeros((4 * LN, LN), F32)
    for c in range(4):
        out += dot(
            onehot((rep == qlane) & (qmod == c)), tile_ref[:, c * LN : (c + 1) * LN]
        )
    msg[...] = out.reshape(DOM, 8, LN).astype(BF16)
    inc[p] = jnp.zeros((8, LN), BF16)
    incb[p] = jnp.zeros((8, LN), BF16)

    pl.semaphore_wait(barrier, DOM - 1 + NX - 1)

    def exchange(src, dst, ss, rs):
        def step(i, last):
            dz = NZ // 2 + (i + 1) // 2 * (1 - 2 * (i % 2))
            for dy in (2, 1, 3, 0):
                for dc in (0, 1):
                    if not last or dy or dc:
                        q = lax.rem(y + dy, NY) * (NZ * NC)
                        q += lax.rem(z + dz, NZ) * NC + lax.rem(core + dc, NC)
                        remote(src.at[q], dst.at[p], ss, rs, q, x).start()

        def loop(i, carry):
            step(i, False)
            return carry

        lax.fori_loop(0, NZ - 1, loop, 0)
        step(NZ - 1, True)

    exchange(msg, inc, r_s, r_r)

    for c in first[2:]:
        c.wait()
    frow = jnp.broadcast_to(from_ref[...], (LN, ND))
    fcol = frow.T
    fcol4 = jnp.concatenate([fcol] * 4, 1)
    for c in range(4):
        gat_i[c * ND : (c + 1) * ND, :] = onehot(
            (fcol4 - ND) * 4 + c == iota((ND, 4 * LN), 1)
        )
    stay = onehot(fcol == iota((ND, LN), 1))

    lane = iota((LN, LN), 1)
    subl = iota((LN, LN), 0)

    def selections(b, carry):
        rows = pl.ds(pl.multiple_of(b * LN, LN), LN)
        srow = jnp.broadcast_to(snd_ref[pl.ds(b, 1), :], (LN, LN))
        rrow = jnp.broadcast_to(rcv_ref[pl.ds(b, 1), :], (LN, LN))
        scol = srow.T
        rcol = rrow.T
        for k in range(TR // LN):
            sel_s[rows, k * LN : (k + 1) * LN] = onehot(scol == lane + k * LN)
            sel_st[k * LN : (k + 1) * LN, rows] = onehot(srow == subl + k * LN)
        r = onehot(rcol == lane)
        sel_r[rows, :LN] = r
        sel_r[rows, LN:] = r
        sel_rt[:, rows] = onehot(rrow == subl)
        return carry

    lax.fori_loop(0, ED // LN, selections, 0)
    table[pl.ds(NX * ND + 32, TR - NX * ND - 32), :] = jnp.zeros((TR - NX * ND - 32, H), BF16)

    loads[0].wait()
    loads[1].wait()

    def edge_term(b, carry):
        rows = pl.ds(pl.multiple_of(b * EF, EF), EF)
        pre[rows, :] = dot(e[rows, :], ein[:H, :])
        return carry

    lax.fori_loop(0, ED // EF, edge_term, 0)

    pltpu.make_async_copy(inc.at[pl.ds(0, DOM - 1)], inc.at[pl.ds(0, DOM - 1)], r_r).wait()
    got = inc[...].astype(F32).reshape(4 * LN, LN).astype(BF16)
    slots = dot(gat_i[...], got)
    latent = jnp.concatenate(
        [
            (
                dot(stay, tile_ref[:, c * LN : (c + 1) * LN])
                + slots[c * ND : (c + 1) * ND, :]
            ).astype(BF16)
            for c in range(4)
        ],
        1,
    )
    lat[...] = latent
    own_rows = pl.ds(pl.multiple_of(x * ND, ND), ND)
    table[own_rows, :] = latent

    half_rows = ND // 2

    def piece(t, part):
        return table.at[pl.ds(pl.multiple_of(t * ND + part * half_rows, half_rows), half_rows)]

    def gather_copy(t, part, j, i):
        return remote(piece(t, part), piece(t, part), a_s.at[i], a_r.at[i], p, xpeer(j))

    def arrived(t, part, i):
        pltpu.make_async_copy(piece(t, part), piece(t, part), a_r.at[i]).wait()

    gathers = [
        gather_copy(x, 0, 1, 0), gather_copy(x, 1, 3, 2),
        gather_copy(x, 1, 1, 1), gather_copy(x, 0, 3, 3),
    ]
    for c in gathers:
        c.start()
    cutb = jnp.broadcast_to(cut_ref[...], (LN, 32)).astype(F32).astype(BF16)
    eye = onehot(iota((32, 32), 0) == iota((32, 32), 1))
    ccol = dot_nt(eye, cutb)
    halo_s[...] = dot(onehot(ccol == iota((32, LN), 1).astype(F32)), latent).astype(BF16)
    halos = [
        remote(halo_s.at[pl.ds(16, 16)], table.at[pl.ds(512, 16)], a_s.at[6], a_r.at[6], up, x),
        remote(halo_s.at[pl.ds(0, 16)], table.at[pl.ds(528, 16)], a_s.at[7], a_r.at[7], dn, x),
    ]
    for c in halos:
        c.start()

    rh, rl = hi_lo(dot(latent, ein[2 * H :, :]))
    recv_proj = jnp.concatenate([rh, rl], 0)

    def recv_term(b, carry):
        rows = pl.ds(pl.multiple_of(b * EF, EF), EF)
        pre[rows, :] += dot(sel_r[rows, :], recv_proj)
        return carry

    lax.fori_loop(0, ED // EF, recv_term, 0)
    prow = dot_nt(pickb, quad)
    pq = iota((ND, 4 * LN), 1) % 4
    pn = iota((ND, 4 * LN), 0).astype(F32)
    frow4 = jnp.broadcast_to(from_ref[...], (4 * LN, ND))
    fq = iota((4 * LN, ND), 0)
    for c in range(4):
        back_o[c * ND : (c + 1) * ND, :] = onehot((prow == pn) & (pq == c))
        back_p[:, c * ND : (c + 1) * ND] = onehot((frow4 - ND) * 4 + c == fq)
    for c in loads[2:]:
        c.wait()
    nbase[...] = dot(latent, nin[:H, :])

    arrived(xpeer(3), 0, 0)
    forwards = [gather_copy(xpeer(3), 0, 1, 4)]
    forwards[0].start()
    arrived(xpeer(1), 1, 2)
    forwards.append(gather_copy(xpeer(1), 1, 3, 5))
    forwards[1].start()
    arrived(xpeer(3), 1, 1)
    arrived(xpeer(1), 0, 3)
    arrived(xpeer(2), 0, 4)
    arrived(xpeer(2), 1, 5)
    for c in halos:
        c.wait_recv()

    def edge_forward(b, carry):
        rows = pl.ds(pl.multiple_of(b * EF, EF), EF)
        send_rows = dot(sel_s[rows, :], table[...]).astype(BF16)
        a, da = silu_pair(pre[rows, :] + dot(send_rows, ein[H : 2 * H, :]))
        a = a.astype(BF16)
        act[rows, :] = a
        dsilu[rows, :] = da
        yn, inv = norm(dot(a, eout[...]))
        normed[rows, :] = yn
        einv[rows, :] = jnp.broadcast_to(inv, (EF, LN))
        enew[rows, :] = (e[rows, :].astype(F32) + yn).astype(BF16)
        return carry

    lax.fori_loop(0, ED // EF, edge_forward, 0)

    agg = dot(sel_rt[...], enew[...]).astype(BF16)
    node_act, node_dsilu = silu_pair(nbase[...] + dot(agg, nin[H:, :]))
    node_act = node_act.astype(BF16)
    nnorm, ninv = norm(dot(node_act, nout[...]))
    nodeup_ref[...] = (latent.astype(F32) + nnorm).astype(BF16)
    ncot = ncot_ref[...].astype(F32)
    nlg = norm_grad(nnorm, ninv, ncot).astype(BF16)
    npg = (dot_nt(nlg, nout[...]) * node_dsilu).astype(BF16)
    agh, agl = hi_lo(dot_nt(npg, nin[H:, :]))
    agg_grad = jnp.concatenate([agh, agl], 0)
    wg[4 * H : 5 * H, :] = dot_tn(latent, npg)
    wg[5 * H : 6 * H, :] = dot_tn(agg, npg)
    wg[6 * H :, :] = dot_tn(node_act, nlg)

    def two_blocks(block, k, side):
        base = 2 * SUB * block + 4 * 56 * k + 56 * side
        return jnp.concatenate(
            [
                wg[pl.ds(pl.multiple_of(base, 8), 56), :],
                wg[pl.ds(pl.multiple_of(base + 112, 8), 56), :],
            ],
            0,
        )

    def core_copy(block):
        rows = pl.ds(SUB * block, SUB)
        return remote(
            csend.at[rows], crecv.at[rows], c_s.at[block], c_r.at[block], sib, x
        )

    def pack_core(block):
        for k in range(2):
            rows = pl.ds(SUB * block + 112 * k, 112)
            csend[rows, :] = two_blocks(block, k, 1 - core).astype(BF16)
        core_copy(block).start()

    def columns(t):
        return pl.ds(pl.multiple_of(t * LN, LN), LN)

    def x1_copy(block, j):
        t = xpeer(j)
        i = 3 * block + j - 1
        return remote(
            chip.at[pl.ds(SUB * block, RX), columns(t)], rx.at[i], x1_s.at[i], x1_r.at[i], p, t
        )

    def y_copy(src, dst, ss, rs, block):
        i = 2 * (lax.rem(block // 2 - y + NY, NY) - 1) + block % 2
        return remote(
            src, dst.at[i], ss.at[i], rs.at[i], p + (block // 2 - y) * NC * NZ, x
        )

    def y1_copy(block):
        return y_copy(chip.at[pl.ds(SUB * block + RX, RY)], ry1, y1_s, y1_r, block)

    def y2_copy(block):
        return y_copy(bx.at[block], ry, y2_s, y2_r, block)

    def x2_copy(s, j):
        t = xpeer(j)
        i = 3 * s + j - 1
        return remote(b1.at[s, :, columns(t)], rx2.at[i], x2_s.at[i], x2_r.at[i], p, t)

    def y_block(j, s):
        return 2 * lax.rem(y + j, NY) + s

    def combine(block):
        core_copy(block).wait_recv()
        for k in range(2):
            rows = pl.ds(SUB * block + 112 * k, 112)
            chip[rows, :] = (
                two_blocks(block, k, core) + crecv[rows, :].astype(F32)
            ).astype(BF16)

        @pl.when(y != block // 2)
        def _():
            y1_copy(block).start()

        for j in (1, 3, 2):
            x1_copy(block, j).start()

    mine = columns(x)

    def finish_x(block):
        total = chip[pl.ds(SUB * block, RX), mine].astype(F32)
        for j in (1, 3, 2):
            x1_copy(block, j).wait_recv()
            total += rx[3 * block + j - 1].astype(F32)
        bx[block] = total.astype(BF16)

        @pl.when(y != block // 2)
        def _():
            y2_copy(block).start()

    def finish_y(s):
        own = pl.ds(pl.multiple_of(SUB * (2 * y + s) + RX, 16), RY)
        total = chip[own, :].astype(F32)
        for j in range(1, NY):
            y1_copy(y_block(j, s)).wait_recv()
            total += ry1[2 * (j - 1) + s].astype(F32)
        b1[s] = total.astype(BF16)
        for j in (1, 3, 2):
            x2_copy(s, j).start()

    for block in (7, 6, 5):
        pack_core(block)

    def edge_backward(b, carry):
        rows = pl.ds(pl.multiple_of(b * EB, EB), EB)
        upst = cot[rows, :].astype(F32) + dot(sel_r[rows, :], agg_grad)
        g = norm_grad(normed[rows, :], einv[rows, :1], upst).astype(BF16)
        plg[rows, :] = g
        pg = (dot_nt(g, eout[...]) * dsilu[rows, :]).astype(BF16)
        ppg[rows, :] = pg
        return carry

    lax.fori_loop(0, ED // EB, edge_backward, 0)
    def own_of(t):
        return pl.ds(pl.multiple_of(t * ND, ND), ND)

    scatters = [
        remote(gs.at[own_of(xpeer(j))], gr.at[j - 1], g_s.at[j], g_r.at[j], p, xpeer(j))
        for j in (1, 3, 2)
    ] + [
        remote(gs.at[pl.ds(512, 16)], hb.at[pl.ds(16, 16)], g_s.at[0], g_r.at[0], dn, x),
        remote(gs.at[pl.ds(528, 16)], hb.at[pl.ds(0, 16)], g_s.at[4], g_r.at[4], up, x),
    ]
    wg[:H, :] = dot_tn(e[...], ppg[...])
    pack_core(0)
    for block in (7, 6, 5):
        combine(block)
    grecv = dot(sel_rt[...], ppg[...]).astype(BF16)
    wg[2 * H : 3 * H, :] = dot_tn(latent, grecv)
    gsum[...] = dot(sel_st[...], ppg[...])
    gs[...] = gsum[...].astype(BF16)
    wg[H : 2 * H, :] = dot_tn(table[...], gs[...])
    pack_core(2)
    pack_core(1)
    wg[3 * H : 4 * H, :] = dot_tn(act[...], plg[...])
    pack_core(3)
    pack_core(4)
    for c in scatters:
        c.start()
    for block in (0, 2, 1, 3, 4):
        combine(block)

    def edge_result(b, carry):
        rows = pl.ds(pl.multiple_of(b * EB, EB), EB)
        total = cot[rows, :].astype(F32) + dot(sel_r[rows, :], agg_grad)
        egrad[rows, :] = (total + dot_nt(ppg[rows, :], ein[:H, :])).astype(BF16)
        return carry

    lax.fori_loop(0, ED // EB, edge_result, 0)
    node_direct = ncot + dot_nt(npg, nin[:H, :])
    node_part = node_direct + dot_nt(grecv, ein[2 * H :, :])

    for c in scatters:
        c.wait_recv()
    crow = jnp.broadcast_to(cut_ref[...], (ND, 32))
    total = dot(onehot(crow == iota((ND, 32), 0)), hb[...])
    total += gsum[own_rows, :]
    for j in range(3):
        total += gr[j].astype(F32)
    node_grad = (node_part + dot_nt(total.astype(BF16), ein[H : 2 * H, :])).astype(BF16)
    ng = jnp.concatenate([node_grad[:, c * LN : (c + 1) * LN] for c in range(4)], 0)
    msgb[...] = dot(back_p[...], ng).reshape(DOM, 8, LN).astype(BF16)

    exchange(msgb, incb, rb_s, rb_r)
    for block in (7, 6, 5):
        finish_x(block)

    def z_copy(t):
        i = lax.rem(t - z + NZ, NZ) - 1
        return remote(zp.at[t], rz.at[i], z_s.at[i], z_r.at[i], p + (t - z) * NC, x)

    def half_sum(s):
        part = bx[2 * y + s].astype(F32)
        for j in range(1, NY):
            y2_copy(y_block(j, s)).wait_recv()
            part += ry[2 * (j - 1) + s].astype(F32)
        rest = b1[s, :, mine].astype(F32)
        for j in (1, 3, 2):
            x2_copy(s, j).wait_recv()
            rest += rx2[3 * s + j - 1].astype(F32)
        total = jnp.concatenate([part, rest], 0)
        zown[SUB * s : SUB * (s + 1), :] = total
        for k in range(4):
            zp[4 * s + k] = jnp.concatenate(
                [total[56 * k : 56 * k + 56, :], jnp.zeros((8, LN), F32)], 0
            ).astype(BF16)
        for k in range(4):
            t = 4 * s + k

            @pl.when(t != z)
            def _():
                z_copy(t).start()

    for block in (0, 2):
        finish_x(block)
    finish_y(0)
    for block in (1, 3, 4):
        finish_x(block)
    finish_y(1)
    half_sum(0)
    half_sum(1)

    pltpu.make_async_copy(incb.at[pl.ds(0, DOM - 1)], incb.at[pl.ds(0, DOM - 1)], rb_r).wait()
    back = incb[...].astype(F32).reshape(4 * LN, LN).astype(BF16)
    slots = dot(back_o[...], back)
    stay_t = onehot(frow == iota((LN, ND), 0))
    latgrad_ref[...] = jnp.concatenate(
        [
            (
                dot(stay_t, node_grad[:, c * LN : (c + 1) * LN])
                + slots[c * ND : (c + 1) * ND, :]
            ).astype(BF16)
            for c in range(4)
        ],
        1,
    )

    total = zown[pl.ds(pl.multiple_of(56 * z, 8), 56), :]
    for j in range(1, NZ):
        z_copy(lax.rem(z + j, NZ)).wait_recv()
        total += rz[j - 1].astype(F32)[:56, :]
    wgrad_ref[...] = total

    pltpu.make_async_copy(msg.at[pl.ds(0, DOM - 1)], msg.at[pl.ds(0, DOM - 1)], r_s).wait()
    pltpu.make_async_copy(msgb.at[pl.ds(0, DOM - 1)], msgb.at[pl.ds(0, DOM - 1)], rb_s).wait()
    for c in gathers + forwards + halos + scatters:
        c.wait_send()
    for block in range(8):
        core_copy(block).wait_send()
        for j in (1, 3, 2):
            x1_copy(block, j).wait_send()
    for s in range(2):
        for j in range(1, NY):
            y1_copy(y_block(j, s)).wait_send()
            y2_copy(y_block(j, s)).wait_send()
            x2_copy(s, j).wait_send()
    for j in range(1, NZ):
        z_copy(lax.rem(z + j, NZ)).wait_send()


def hand_over(*refs):
    sem = refs[-1]
    copies = [
        pltpu.make_async_copy(a, b, sem.at[i])
        for i, (a, b) in enumerate(zip(refs[:5], refs[5:10]))
    ]
    for c in copies:
        c.start()
    for c in copies:
        c.wait()


def body(
    tile_latent, relay_pick, relay_from, cut_pick, edge_latent, edge_sender, edge_receiver,
    edge_in, edge_out, node_in, node_out, node_cot, edge_cot,
):
    vmem = pl.BlockSpec(memory_space=pltpu.VMEM)
    hbm = pl.BlockSpec(memory_space=pl.ANY)
    pin = pl.BlockSpec(memory_space=pltpu.HBM)
    dma = pltpu.SemaphoreType.DMA
    V = pltpu.VMEM
    scratch = [
        V((ED, H), BF16), V((ED, H), BF16), V((3 * H, H), BF16), V((H, H), BF16),
        V((2 * H, H), BF16), V((H, H), BF16), V((ND, H), BF16), V((1, LN), jnp.int32),
        V((1, ND), jnp.int32), V((ED // LN, LN), jnp.int32), V((ED // LN, LN), jnp.int32),
        V((ND, H), BF16), dma((12,)), V((ND, H), F32),
        V((DOM, 8, LN), BF16), V((DOM, 8, LN), BF16), V((DOM, 8, LN), BF16), V((DOM, 8, LN), BF16),
        V((TR, H), BF16), V((ND, H), BF16), V((32, H), BF16),
        V((ED, TR), BF16), V((TR, ED), BF16), V((ED, 2 * LN), BF16), V((ND, ED), BF16),
        V((4 * ND, 4 * LN), BF16), V((4 * ND, 4 * LN), BF16), V((4 * LN, 4 * ND), BF16),
        V((ED, H), F32), V((ED, H), BF16), V((ED, H), F32), V((ED, H), F32), V((ED, LN), F32),
        V((ED, H), BF16), V((ED, H), BF16),
        V((TR, H), F32), V((TR, H), BF16), V((3, ND, H), BF16), V((32, H), BF16), V((7 * H, H), F32),
        V((8 * SUB, H), BF16), V((8 * SUB, H), BF16), V((8 * SUB, H), BF16),
        V((24, RX, LN), BF16), V((8, RX, LN), BF16), V((6, RX, LN), BF16),
        V((6, RY, H), BF16), V((2, RY, H), BF16), V((6, RY, LN), BF16),
        V((2 * SUB, LN), F32), V((NZ, 64, LN), BF16), V((NZ - 1, 64, LN), BF16),
        dma, dma, dma((8,)), dma((8,)), dma, dma, dma((5,)), dma((5,)), dma((8,)), dma((8,)),
        dma((24,)), dma((24,)), dma((6,)), dma((6,)), dma((6,)), dma((6,)), dma((6,)), dma((6,)),
        dma((NZ - 1,)), dma((NZ - 1,)),
    ]
    held = tuple(
        pltpu.VMEM(s, d)
        for s, d in (
            ((ND, H), BF16), ((ED, H), BF16), ((ND, H), BF16), ((ED, H), BF16), ((56, LN), F32),
        )
    )
    shapes = (
        jax.ShapeDtypeStruct((ND, H), BF16),
        jax.ShapeDtypeStruct((ED, H), BF16),
        jax.ShapeDtypeStruct((ND, H), BF16),
        jax.ShapeDtypeStruct((ED, H), BF16),
        jax.ShapeDtypeStruct((56, LN), F32),
    )
    parts = pl.pallas_call(
        kernel,
        out_shape=held,
        in_specs=[pin] * 3 + [vmem] + [pin] * 3 + [hbm] * 6,
        out_specs=(vmem,) * 5,
        scratch_shapes=scratch,
        compiler_params=pltpu.CompilerParams(
            collective_id=0, has_side_effects=True, vmem_limit_bytes=56 * 2**20
        ),
    )(
        tile_latent, relay_pick, relay_from.reshape(1, ND), cut_pick,
        edge_sender.reshape(ED // LN, LN), edge_receiver.reshape(ED // LN, LN), node_cot,
        edge_latent, edge_cot, edge_in, edge_out, node_in, node_out,
    )
    return pl.pallas_call(
        hand_over,
        out_shape=shapes,
        in_specs=[vmem] * 5,
        out_specs=(hbm,) * 5,
        scratch_shapes=[dma((5,))],
        compiler_params=pltpu.CompilerParams(vmem_limit_bytes=2**20),
    )(*parts)


def solution(mesh):
    rows = P(("dom", "tile"), None)
    flat = P(("dom", "tile"))
    in_specs = (
        rows, rows, flat, rows, rows, flat, flat, P(), P(), P(), P(), rows, rows,
    )
    out_specs = (rows, rows, rows, rows, P("dom", "tile"))
    return jax.shard_map(body, mesh=mesh, in_specs=in_specs, out_specs=out_specs, check_vma=False)
```
